32 devices in a mesh: row: 4 (over z), col: 8 (over y, x, core).
Axes of the slice: x: 2, y: 2, z: 4, core: 2. Of those that a mesh axis runs over, the one named last changes fastest.
Arguments:
- matrix: float32 [16384, 16384], P('row', 'col'), may hold values from -48 to 48, as said below
- pivots: int32 [2, 64], replicated, may hold values from 128 to 16383, as said below
Outputs:
- factored: float32 [16384, 16384], P('row', 'col')
The draws below stay inside these ranges and needn't reach their ends.
Inputs may be any that keep to these rules, and one draw needn't show every extreme that they name: `pivots`: the 128 entries are distinct global row numbers. `matrix`: the entry of row pivots[c, k] in global column c * 64 + k dominates the other entries of its global column, so that multipliers stay well below one.
All inputs are finite; a program needn't handle non-finite values.
Results may differ from the reference program's by a relative error of at most 0.0002.
Values sent between devices are 32-bit elements; how exact they have to be, the bound alone decides.
No kernel may reach another device: no remote copies, remote signals or barrier semaphores. Data moves between devices by JAX's collectives and lax.ppermute only.
A program may use at most 128 MiB of HBM per device.

```python
import math
import jax
import jax.numpy as jnp
from jax import lax

NB = 64
ORDER = 16384
BLK_ROWS = 64
BLK_COLS = 32
N_ROW = 4
N_COL = 8


def pivot_rows(key):
    sub_key = jax.random.fold_in(key, 11)
    chosen = jax.random.permutation(sub_key, ORDER - 2 * NB)[:2 * NB] + 2 * NB
    return chosen.astype(jnp.int32)


def draw_pivots(key, part):
    return pivot_rows(key).reshape(2, NB)


def draw_matrix(key, part):
    grid_rows = ORDER // (NB * BLK_ROWS)
    grid_cols = ORDER // (NB * BLK_COLS)
    key_values = jax.random.fold_in(key, 21)
    key_sizes = jax.random.fold_in(key, 23)
    key_signs = jax.random.fold_in(key, 24)
    values = 0.4 * jax.random.truncated_normal(key_values, -4.0, 4.0, (ORDER, ORDER), jnp.float32)
    chosen = pivot_rows(key)
    magnitudes = jnp.exp(jax.random.uniform(key_sizes, (2 * NB,), jnp.float32, math.log(16.0), math.log(48.0)))
    sign_values = jnp.where(jax.random.bernoulli(key_signs, 0.5, (2 * NB,)), 1.0, -1.0)
    values = values.at[chosen, jnp.arange(2 * NB)].set(magnitudes * sign_values)
    values = values.reshape(BLK_ROWS, grid_rows, NB, BLK_COLS, grid_cols, NB)
    return values.transpose(1, 0, 2, 4, 3, 5).reshape(ORDER, ORDER)


def setup_inputs(seed: int = 0) -> dict:
    seeds = jax.random.split(jax.random.key(seed), 3)
    return {
        "matrix": draw_matrix(jax.random.fold_in(seeds[2], 71), 0),
        "pivots": draw_pivots(jax.random.fold_in(seeds[2], 71), 0),
    }


HIGHEST_PRECISION = lax.Precision.HIGHEST

def eliminate(panel_t):
    panel_width, row_count = panel_t.shape
    row_ids = jnp.arange(row_count, dtype=jnp.int32)
    col_ids = jnp.arange(panel_width, dtype=jnp.int32)

    def eliminate_step(column, current):
        pivot_line = lax.dynamic_index_in_dim(current, column, 1, keepdims=False)
        pivot_value = lax.dynamic_index_in_dim(pivot_line, column, 0, keepdims=False)
        weight = 1.0 / pivot_value
        column_line = lax.dynamic_index_in_dim(current, column, 0, keepdims=False)
        below_rows = row_ids > column
        multiplier = jnp.where(below_rows, column_line * weight, 0.0)
        later_part = jnp.where(col_ids > column, pivot_line, 0.0)
        current = current - later_part[:, None] * multiplier[None, :]
        return jnp.where((col_ids == column)[:, None] & below_rows[None, :], multiplier[None, :], current)
    return lax.fori_loop(0, panel_width, eliminate_step, panel_t)

def solve_rows(top_t, right_side):
    unit_part = jnp.tril(top_t.T, -1) + jnp.eye(top_t.shape[0], dtype=top_t.dtype)
    return lax.linalg.triangular_solve(unit_part, right_side, left_side=True, lower=True, unit_diagonal=True)

def reference(matrix, pivots):
    grid_rows = N_ROW
    grid_cols = N_COL
    whole_matrix = matrix.reshape(grid_rows, BLK_ROWS, NB, grid_cols, BLK_COLS, NB)
    whole_matrix = whole_matrix.transpose(1, 0, 2, 4, 3, 5).reshape(ORDER, ORDER)
    top_global = jnp.arange(2 * NB, dtype=jnp.int32)
    pivot_global = pivots.reshape(-1).astype(jnp.int32)
    order_index = jnp.arange(ORDER, dtype=jnp.int32).at[top_global].set(pivot_global).at[pivot_global].set(top_global)
    whole_matrix = whole_matrix[order_index]
    for panel in range(2):
        first_row = panel * NB
        factored_panel = eliminate(whole_matrix[first_row:, first_row:first_row + NB].T)
        whole_matrix = whole_matrix.at[first_row:, first_row:first_row + NB].set(factored_panel.T)
        upper_rows = solve_rows(factored_panel[:, :NB], whole_matrix[first_row:first_row + NB, first_row + NB:])
        whole_matrix = whole_matrix.at[first_row:first_row + NB, first_row + NB:].set(upper_rows)
        product = lax.dot_general(factored_panel[:, NB:].astype(jnp.float32), upper_rows.astype(jnp.float32), (((0,), (0,)), ((), ())), precision=HIGHEST_PRECISION, preferred_element_type=jnp.float32)
        whole_matrix = whole_matrix.at[first_row + NB:, first_row + NB:].set(whole_matrix[first_row + NB:, first_row + NB:] - product)
    result = whole_matrix.reshape(BLK_ROWS, grid_rows, NB, BLK_COLS, grid_cols, NB)
    return result.transpose(1, 0, 2, 4, 3, 5).reshape(ORDER, ORDER)
```

```python
import functools

import jax
import jax.numpy as jnp
from jax import lax
from jax.experimental import pallas as pl
from jax.experimental.pallas import tpu as pltpu
from jax.sharding import PartitionSpec as P

NB = 64
NP = 2 * NB
LANES = 128
SUB = 8
HIGHEST_PRECISION = lax.Precision.HIGHEST
MIB = 1024 * 1024


def capacities(grid_rows):
    cap = min(NP, -(-3 * NP // (2 * grid_rows * SUB)) * SUB)
    cap_top = min(NB, -(-2 * NB // (grid_rows * SUB)) * SUB)
    return cap, cap_top


def owner_of(row, grid_rows):
    return lax.rem(lax.div(row, NB), grid_rows)


def local_of(row, grid_rows):
    return lax.div(row, NB * grid_rows) * NB + lax.rem(row, NB)


def split(x):
    high = x.astype(jnp.bfloat16)
    return high, (x - high.astype(jnp.float32)).astype(jnp.bfloat16)


def mm(a, b):
    return jnp.dot(a, b, preferred_element_type=jnp.float32)


def gather_kernel(grid_rows, where_ref, piv_ref, m_ref, rows_ref, corner_ref, _, line_ref, sem):
    my_row = where_ref[0]
    cap = rows_ref.shape[0]
    line_ref[...] = jnp.zeros_like(line_ref)

    def line_copy(row, t):
        return pltpu.make_async_copy(
            m_ref.at[pl.ds(row, 1), pl.ds(0, LANES)], line_ref.at[pl.ds(t, 1), :], sem.at[0]
        )

    def row_copy(row, slot):
        return pltpu.make_async_copy(
            m_ref.at[pl.ds(row, 1), :], rows_ref.at[pl.ds(slot, 1), :], sem.at[1]
        )

    def start(t, count):
        row = piv_ref[t]
        mine = owner_of(row, grid_rows) == my_row

        @pl.when(mine)
        def _():
            line_copy(local_of(row, grid_rows), t).start()

        @pl.when(mine & (count < cap))
        def _():
            row_copy(local_of(row, grid_rows), count).start()

        return count + mine.astype(jnp.int32)

    count = lax.fori_loop(0, NP, start, jnp.int32(0))

    def wait_line(_, carry):
        line_copy(0, 0).wait()
        return carry

    def wait_row(_, carry):
        row_copy(0, 0).wait()
        return carry

    lax.fori_loop(0, count, wait_line, 0)
    lane = lax.broadcasted_iota(jnp.int32, (NB, LANES), 1)
    corner_ref[...] = jnp.where(lane < NB, line_ref[:NB], pltpu.roll(line_ref[NB:], NB, 1))
    lax.fori_loop(0, jnp.minimum(count, cap), wait_row, 0)


def gather_rows(matrix, pivots, where, cap, grid_rows):
    cols = matrix.shape[1]
    smem = pl.BlockSpec(memory_space=pltpu.SMEM)
    vmem = pl.BlockSpec(memory_space=pltpu.VMEM)
    anywhere = pl.BlockSpec(memory_space=pl.ANY)
    return pl.pallas_call(
        functools.partial(gather_kernel, grid_rows),
        out_shape=(
            jax.ShapeDtypeStruct((cap, cols), jnp.float32),
            jax.ShapeDtypeStruct((NB, LANES), jnp.float32),
            jax.ShapeDtypeStruct((NP, cols), jnp.float32),
        ),
        in_specs=[smem, smem, anywhere],
        out_specs=(vmem, vmem, anywhere),
        scratch_shapes=[pltpu.VMEM((NP, LANES), jnp.float32), pltpu.SemaphoreType.DMA((2,))],
        compiler_params=pltpu.CompilerParams(vmem_limit_bytes=16 * MIB),
        name="gather_rows",
    )(where, pivots, matrix)


def pack_kernel(top_ref, bottom_ref, out_ref):
    lane = lax.broadcasted_iota(jnp.int32, out_ref.shape, 1)
    out_ref[...] = jnp.where(lane < NB, top_ref[...], pltpu.roll(bottom_ref[...], NB, 1))


def pack_panel(matrix, steps):
    half = matrix.shape[0] // 2
    size = half // steps
    return pl.pallas_call(
        pack_kernel,
        out_shape=jax.ShapeDtypeStruct((half, LANES), jnp.float32),
        grid=(steps,),
        in_specs=[
            pl.BlockSpec((size, LANES), lambda i: (i, 0)),
            pl.BlockSpec((size, LANES), lambda i: (i + steps, 0)),
        ],
        out_specs=pl.BlockSpec((size, LANES), lambda i: (i, 0)),
        compiler_params=pltpu.CompilerParams(vmem_limit_bytes=16 * MIB),
        name="pack_panel",
    )(matrix, matrix)


GROUP = 4


def eliminate_in_place(work, lane, sub):
    count = len(work)
    work = list(work)
    shape = work[0].shape
    for first in range(0, NP, GROUP):
        block, inner = divmod(first, SUB)
        below = list(range(block, count))
        cols = [
            {i: jnp.broadcast_to(work[i][:, first + j : first + j + 1], shape) for i in below}
            for j in range(GROUP)
        ]
        rows = [
            jnp.broadcast_to(work[block][inner + j : inner + j + 1, :], shape)
            for j in range(GROUP)
        ]
        spots = [
            [jnp.broadcast_to(cols[j][block][inner + i : inner + i + 1, :], shape) for j in range(GROUP)]
            for i in range(GROUP)
        ]
        scaled = []
        for j in range(GROUP):
            weight = 1.0 / spots[j][j]
            at_j = lane == first + j
            line = jnp.where(at_j, 1.0, rows[j]) * weight
            factor = {l: spots[j][l] * weight for l in range(j + 1, GROUP)}
            for i in range(j + 1, GROUP):
                rows[i] = jnp.where(at_j, 0.0, rows[i]) - spots[i][j] * line
                for l in range(j + 1, GROUP):
                    spots[i][l] = spots[i][l] - spots[i][j] * factor[l]
            for l in range(j + 1, GROUP):
                for i in below:
                    cols[l][i] = cols[l][i] - cols[j][i] * factor[l]
            later = (lane > first + j) & (lane < first + GROUP)
            scaled.append(jnp.where(later, 0.0, line))
        in_group = (lane >= first) & (lane < first + GROUP)
        for i in below:
            updated = jnp.where(in_group, 0.0, work[i])
            for j in range(GROUP):
                updated = updated - cols[j][i] * scaled[j]
            if i == block:
                updated = jnp.where(sub < inner, work[i], updated)
                for j in range(GROUP):
                    updated = jnp.where(sub == inner + j, rows[j], updated)
            work[i] = updated
    return work


def corner_kernel(where_ref, mine_ref, other_ref, lu_ref, linv_ref, weights_ref):
    my_col = where_ref[1]
    odd = lax.rem(my_col, 2) == 1
    even_part = jnp.where(odd, other_ref[...], mine_ref[...])
    odd_part = jnp.where(odd, mine_ref[...], other_ref[...])
    left = lax.broadcasted_iota(jnp.int32, (NB, LANES), 1) < NB
    a = jnp.concatenate(
        [
            jnp.where(left, even_part, pltpu.roll(odd_part, NB, 1)),
            jnp.where(left, pltpu.roll(even_part, NB, 1), odd_part),
        ],
        axis=0,
    )
    a_t = a.T
    lane = lax.broadcasted_iota(jnp.int32, (SUB, LANES), 1)
    sub = lax.broadcasted_iota(jnp.int32, (SUB, LANES), 0)
    blocks = range(0, NP, SUB)
    first = eliminate_in_place([a[i : i + SUB] for i in blocks], lane, sub)
    second = eliminate_in_place([a_t[i : i + SUB] for i in blocks], lane, sub)
    w1 = jnp.concatenate(first, axis=0)
    w2 = jnp.concatenate(second, axis=0)
    row = lax.broadcasted_iota(jnp.int32, (NP, NP), 0)
    col = lax.broadcasted_iota(jnp.int32, (NP, NP), 1)
    inverse_d = 1.0 / jnp.sum(jnp.where(row == col, w1, 0.0), axis=0, keepdims=True)
    linv_ref[...] = jnp.where(row > col, w1, jnp.where(row == col, 1.0, 0.0))
    w2_t = w2.T
    lu = jnp.where(row <= col, w1, w2_t * inverse_d)
    lu_ref[...] = jnp.where(my_col == 1, pltpu.roll(lu, NB, 1), lu)
    uinv = jnp.where(row < col, w2_t, jnp.where(row == col, 1.0, 0.0)) * inverse_d
    mine = jnp.where(odd, uinv[NB:], uinv[:NB])
    other = jnp.where(odd, uinv[:NB], uinv[NB:])
    zero = jnp.zeros_like(mine)
    weights_ref[0] = jnp.concatenate([mine, zero, other, zero], axis=0)
    weights_ref[1] = jnp.concatenate([zero, mine, zero, other], axis=0)


def assemble(grid_rows, my_row, piv_ref, piece_refs, out_ref, count_ref):
    for r in range(grid_rows):
        count_ref[r] = 0

    def place(t, carry):
        owner = owner_of(piv_ref[t], grid_rows)
        slot = count_ref[owner]
        count_ref[owner] = slot + 1
        back = lax.rem(my_row - owner + grid_rows, grid_rows)
        for s in range(grid_rows):

            @pl.when(back == s)
            def _(s=s):
                out_ref[pl.ds(t, 1), :] = piece_refs[s][pl.ds(slot, 1), :]

        return carry

    lax.fori_loop(0, NP, place, 0)


def factor_corner(mine, other, where):
    smem = pl.BlockSpec(memory_space=pltpu.SMEM)
    vmem = pl.BlockSpec(memory_space=pltpu.VMEM)
    square = jax.ShapeDtypeStruct((NP, NP), jnp.float32)
    return pl.pallas_call(
        corner_kernel,
        out_shape=(square, square, jax.ShapeDtypeStruct((2, 2 * NP, NP), jnp.float32)),
        in_specs=[smem, vmem, vmem],
        out_specs=(vmem, vmem, vmem),
        compiler_params=pltpu.CompilerParams(vmem_limit_bytes=24 * MIB),
        name="factor_corner",
    )(where, mine, other)


def upper_kernel(grid_rows, where_ref, piv_ref, *refs):
    piece_refs = refs[:grid_rows]
    all_ref, linv_ref, lu_ref, high_ref, low_ref, top_ref, a_ref, count_ref, sem = refs[grid_rows:]
    my_row = where_ref[0]
    my_col = where_ref[1]

    @pl.when(where_ref[2] == 0)
    def _():
        assemble(grid_rows, my_row, piv_ref, piece_refs, a_ref, count_ref)

    @pl.when(where_ref[2] != 0)
    def _():
        copy = pltpu.make_async_copy(all_ref, a_ref, sem)
        copy.start()
        copy.wait()

    cols = a_ref.shape[1]
    width = min(cols, 512)
    linv_high, linv_low = split(linv_ref[...])
    linv_both = jnp.concatenate([linv_high, linv_low], axis=1)
    for start in range(0, cols, width):
        span = slice(start, start + width)
        a_high, a_low = split(a_ref[:, span])
        a_ref[:, span] = mm(linv_both, jnp.concatenate([a_high, a_high], axis=0)) + mm(
            linv_high, a_low
        )

    @pl.when(my_row == 0)
    def _():
        top_ref[...] = a_ref[:NB]

    @pl.when(my_row != 0)
    def _():
        top_ref[...] = a_ref[NB:]

    @pl.when(my_col < 2)
    def _():
        lane = lax.broadcasted_iota(jnp.int32, (NP, LANES), 1)
        row = lax.broadcasted_iota(jnp.int32, (NP, LANES), 0)
        lu_part = jnp.where(my_row == 0, lu_ref[:NB], lu_ref[NB:])
        top_ref[:, :LANES] = jnp.where(lane[:NB] < NB, lu_part, top_ref[:, :LANES])
        unit = jnp.where(row == lane + my_col * NB, -1.0, 0.0)
        a_ref[:, :LANES] = jnp.where(lane < NB, unit, a_ref[:, :LANES])

    high, low = split(a_ref[...])
    high_ref[...] = high
    low_ref[...] = low


def upper_rows_of(pieces, everything, linv, lu, pivots, where, grid_rows):
    cols = pieces[0].shape[1]
    smem = pl.BlockSpec(memory_space=pltpu.SMEM)
    vmem = pl.BlockSpec(memory_space=pltpu.VMEM)
    return pl.pallas_call(
        functools.partial(upper_kernel, grid_rows),
        out_shape=(
            jax.ShapeDtypeStruct((NP, cols), jnp.bfloat16),
            jax.ShapeDtypeStruct((NP, cols), jnp.bfloat16),
            jax.ShapeDtypeStruct((NB, cols), jnp.float32),
        ),
        in_specs=[smem, smem] + [vmem] * grid_rows + [pl.BlockSpec(memory_space=pl.ANY), vmem, vmem],
        out_specs=(vmem, vmem, vmem),
        scratch_shapes=[
            pltpu.VMEM((NP, cols), jnp.float32),
            pltpu.SMEM((grid_rows,), jnp.int32),
            pltpu.SemaphoreType.DMA(()),
        ],
        compiler_params=pltpu.CompilerParams(vmem_limit_bytes=32 * MIB),
        name="upper_rows",
    )(where, pivots, *pieces, everything, linv, lu)


def updated_rows(a_ref, panel, weights, high_ref, low_ref, out_ref, is_panel):
    rows, cols = out_ref.shape
    p_high, p_low = split(panel)
    w_high, w_low = split(weights)
    lower = mm(p_high, w_high) + (mm(p_high, w_low) + mm(p_low, w_high))
    l_high, l_low = split(lower)
    both = jnp.concatenate([l_high, l_low], axis=1)
    width = min(cols, 512)
    lane = lax.broadcasted_iota(jnp.int32, (rows, LANES), 1)
    for start in range(0, cols, width):
        span = slice(start, start + width)
        high = high_ref[:, span]
        product = mm(both, jnp.concatenate([high, high], axis=0)) + mm(l_high, low_ref[:, span])
        a = a_ref[:, span]
        if start == 0:
            first = jnp.where((lane < NB) & is_panel, 0.0, a[:, :LANES])
            if width > LANES:
                a = jnp.concatenate([first, a[:, LANES:]], axis=1)
            else:
                a = first
        out_ref[:, span] = a - product


def moved_kernel(grid_rows, cap_top, where_ref, piv_ref, m_ref, own_ref, other_ref, weights_ref, high_ref, low_ref, out_ref, packed_ref, count_ref):
    my_row = where_ref[0]
    panel = jnp.concatenate([own_ref[...], other_ref[...]], axis=1)
    updated_rows(m_ref, panel, weights_ref[0], high_ref, low_ref, out_ref, where_ref[1] < 2)
    for r in range(grid_rows):
        count_ref[r] = 0

    @pl.when(my_row < 2)
    def _():
        def place(k, carry):
            owner = owner_of(piv_ref[my_row * NB + k], grid_rows)
            slot = count_ref[owner]
            count_ref[owner] = slot + 1
            ahead = lax.rem(owner - my_row + grid_rows, grid_rows)

            @pl.when((ahead > 0) & (slot < cap_top))
            def _():
                packed_ref[ahead - 1, pl.ds(slot, 1), :] = out_ref[pl.ds(k, 1), :]

            return carry

        lax.fori_loop(0, NB, place, 0)


def moved_rows(matrix, own, other, weights, high, low, pivots, where, cap_top, grid_rows):
    cols = matrix.shape[1]
    smem = pl.BlockSpec(memory_space=pltpu.SMEM)
    vmem = pl.BlockSpec(memory_space=pltpu.VMEM)
    head = lambda width: pl.BlockSpec((NB, width), lambda i: (0, 0))
    return pl.pallas_call(
        functools.partial(moved_kernel, grid_rows, cap_top),
        out_shape=(
            jax.ShapeDtypeStruct((NB, cols), jnp.float32),
            jax.ShapeDtypeStruct((grid_rows - 1, cap_top, cols), jnp.float32),
        ),
        grid=(1,),
        in_specs=[smem, smem, head(cols), head(LANES), head(LANES), vmem, vmem, vmem],
        out_specs=(
            pl.BlockSpec((NB, cols), lambda i: (0, 0)),
            pl.BlockSpec((grid_rows - 1, cap_top, cols), lambda i: (0, 0, 0)),
        ),
        scratch_shapes=[pltpu.SMEM((grid_rows,), jnp.int32)],
        compiler_params=pltpu.CompilerParams(vmem_limit_bytes=32 * MIB),
        name="moved_rows",
    )(where, pivots, matrix, own, other, weights, high, low)


def trailing_kernel(blocks, where_ref, m_ref, own1, own2, other1, other2, weights_ref, high_ref, low_ref, out_ref, panel_ref):
    step = pl.program_id(0)
    rows = m_ref.shape[0]
    quarter = blocks // 4
    inside = lax.rem(step, quarter)
    part = lax.div(step, quarter)
    here = pl.ds(pl.multiple_of(inside * rows, rows), rows)

    @pl.when(lax.rem(part, 2) == 0)
    def _():
        panel_ref[:, :LANES] = own1[here, :]
        panel_ref[:, LANES:] = other1[here, :]

    @pl.when(lax.rem(part, 2) == 1)
    def _():
        panel_ref[:, :LANES] = own2[here, :]
        panel_ref[:, LANES:] = other2[here, :]

    weights = weights_ref[lax.div(part, 2)]
    updated_rows(m_ref, panel_ref[...], weights, high_ref, low_ref, out_ref, where_ref[1] < 2)


def trailing(matrix, own, other, weights, high, low, where):
    rows, cols = matrix.shape
    size = min(256, rows // 4)
    blocks = rows // size
    smem = pl.BlockSpec(memory_space=pltpu.SMEM)
    vmem = pl.BlockSpec(memory_space=pltpu.VMEM)
    return pl.pallas_call(
        functools.partial(trailing_kernel, blocks),
        out_shape=jax.ShapeDtypeStruct((rows, cols), jnp.float32),
        grid=(blocks,),
        in_specs=[smem, pl.BlockSpec((size, cols), lambda i: (i, 0))] + [vmem] * 7,
        out_specs=pl.BlockSpec((size, cols), lambda i: (i, 0)),
        scratch_shapes=[pltpu.VMEM((size, 2 * LANES), jnp.float32)],
        compiler_params=pltpu.CompilerParams(vmem_limit_bytes=40 * MIB),
        cost_estimate=pl.CostEstimate(
            flops=6 * rows * cols * NP, bytes_accessed=8 * rows * cols, transcendentals=0
        ),
        name="trailing",
    )(where, matrix, own[0], own[1], other[0], other[1], weights, high, low)


def place_kernel(grid_rows, where_ref, piv_ref, *refs):
    moved_refs = refs[:grid_rows]
    all_ref, top_ref, _, out_ref, sem, count_ref = refs[grid_rows:]
    my_row = where_ref[0]
    packed = where_ref[2] == 0

    @pl.when(my_row < 2)
    def _():
        pltpu.make_async_copy(top_ref, out_ref.at[pl.ds(0, NB), :], sem).start()

    count_ref[0] = 0
    count_ref[1] = 0

    def put(t, total):
        row = piv_ref[t]
        mine = owner_of(row, grid_rows) == my_row
        source = lax.div(t, NB)
        back = lax.rem(my_row - source + grid_rows, grid_rows)
        slot = count_ref[source]
        count_ref[source] = slot + mine.astype(jnp.int32)
        to = pl.ds(local_of(row, grid_rows), 1)

        @pl.when(mine & ~packed)
        def _():
            pltpu.make_async_copy(all_ref.at[pl.ds(t, 1), :], out_ref.at[to, :], sem).start()

        @pl.when(mine & packed & (back == 0))
        def _():
            pltpu.make_async_copy(
                moved_refs[0].at[pl.ds(lax.rem(t, NB), 1), :], out_ref.at[to, :], sem
            ).start()

        for s in range(1, grid_rows):

            @pl.when(mine & packed & (back == s))
            def _(s=s):
                pltpu.make_async_copy(
                    moved_refs[s].at[pl.ds(slot, 1), :], out_ref.at[to, :], sem
                ).start()

        return total + mine.astype(jnp.int32)

    total = lax.fori_loop(0, NP, put, jnp.int32(0))

    def wait(_, carry):
        pltpu.make_async_copy(
            moved_refs[0].at[pl.ds(0, 1), :], out_ref.at[pl.ds(0, 1), :], sem
        ).wait()
        return carry

    lax.fori_loop(0, total, wait, 0)

    @pl.when(my_row < 2)
    def _():
        pltpu.make_async_copy(top_ref, out_ref.at[pl.ds(0, NB), :], sem).wait()


def place_moved(moved, everything, top, result, pivots, where, grid_rows):
    smem = pl.BlockSpec(memory_space=pltpu.SMEM)
    anywhere = pl.BlockSpec(memory_space=pl.ANY)
    return pl.pallas_call(
        functools.partial(place_kernel, grid_rows),
        out_shape=jax.ShapeDtypeStruct(result.shape, result.dtype),
        in_specs=[smem, smem] + [anywhere] * (grid_rows + 3),
        out_specs=anywhere,
        input_output_aliases={grid_rows + 4: 0},
        scratch_shapes=[pltpu.SemaphoreType.DMA(()), pltpu.SMEM((2,), jnp.int32)],
        compiler_params=pltpu.CompilerParams(vmem_limit_bytes=16 * MIB),
        name="place_moved",
    )(where, pivots, *moved, everything, top, result)


def spread_chips(value, order, my_chip, chips):
    reached = [0]
    for bit in order:
        pairs = [(2 * c + k, 2 * (c | bit) + k) for c in reached for k in range(2)]
        arrived = lax.ppermute(value, "col", pairs)
        value = jnp.where((my_chip & bit) != 0, arrived, value)
        reached = reached + [c | bit for c in reached]
    return value


def shards(matrix, pivots):
    grid_rows = lax.axis_size("row")
    grid_cols = lax.axis_size("col")
    chips = grid_cols // 2
    assert grid_rows > 1 and chips * 2 == grid_cols and not chips & (chips - 1)
    my_row = lax.axis_index("row")
    my_col = lax.axis_index("col")
    my_chip = my_col // 2
    cap, cap_top = capacities(grid_rows)
    flat = pivots.reshape(-1)
    owner = owner_of(flat, grid_rows)
    owned = jnp.sum(
        owner.reshape(2, NB)[:, :, None] == jnp.arange(grid_rows, dtype=jnp.int32), axis=1
    )
    over = (jnp.max(jnp.sum(owned, axis=0)) > cap) | (jnp.max(owned) > cap_top)
    over = over.astype(jnp.int32)
    where = jnp.stack([my_row, my_col, over]).astype(jnp.int32)
    swap = [(c, c ^ 1) for c in range(grid_cols)]
    shifts = [[(r, (r + s) % grid_rows) for r in range(grid_rows)] for s in range(1, grid_rows)]
    bits = [1 << b for b in range(chips.bit_length() - 1)]

    rows, corner, unwritten = gather_rows(matrix, flat, where, cap, grid_rows)
    corner = corner + sum(lax.ppermute(corner, "row", shift) for shift in shifts)
    corner = jnp.where(my_chip == 0, corner, 0.0) + sum(
        lax.ppermute(corner, "col", [(0, 2 * chip), (1, 2 * chip + 1)]) for chip in range(1, chips)
    )
    corner_other = lax.ppermute(corner, "col", swap)

    packed = pack_panel(matrix, 2)
    quarter = packed.shape[0] // 2
    own = (
        spread_chips(packed[:quarter], bits, my_chip, chips),
        spread_chips(packed[quarter:], bits[::-1], my_chip, chips),
    )
    other = tuple(lax.ppermute(x, "col", swap) for x in own)

    pieces = [rows] + [lax.ppermute(rows, "row", shift) for shift in shifts]

    def sum_rows(state):
        local = jnp.where(owner == my_row, local_of(flat, grid_rows), 0)
        picked = jnp.where((owner == my_row)[:, None], matrix[local], 0.0)
        return jnp.int32(0), lax.psum(picked, "row")

    everything = lax.while_loop(lambda state: state[0] > 0, sum_rows, (over, unwritten))[1]

    lu, linv, weights = factor_corner(corner, corner_other, where)
    high, low, top = upper_rows_of(pieces, everything, linv, lu, flat, where, grid_rows)
    kept, leaving = moved_rows(
        matrix, own[0], other[0], weights, high, low, flat, where, cap_top, grid_rows
    )
    moved = [kept]
    for s in range(1, grid_rows):
        pairs = [(c, (c + s) % grid_rows) for c in range(2)]
        moved.append(lax.ppermute(leaving[s - 1], "row", pairs))

    def sum_moved(state):
        halves = [jnp.where(my_row == c, kept, 0.0) for c in range(2)]
        return jnp.int32(0), lax.psum(jnp.concatenate(halves, axis=0), "row")

    everything = lax.while_loop(lambda state: state[0] > 0, sum_moved, (over, everything))[1]
    result = trailing(matrix, own, other, weights, high, low, where)
    return place_moved(moved, everything, top, result, flat, where, grid_rows)


def solution(mesh):
    placed = (P("row", "col"), P())
    return jax.shard_map(
        shards, mesh=mesh, in_specs=placed, out_specs=P("row", "col"), check_vma=False
    )
```

```python
import functools

import jax
import jax.numpy as jnp
from jax import lax
from jax.experimental import pallas as pl
from jax.experimental.pallas import tpu as pltpu
from jax.sharding import PartitionSpec as P

NB = 64
NP = 2 * NB
LANES = 128
SUB = 8
HIGHEST_PRECISION = lax.Precision.HIGHEST
MIB = 1024 * 1024


def capacities(grid_rows):
    cap = min(NP, -(-3 * NP // (2 * grid_rows * SUB)) * SUB)
    cap_top = min(NB, -(-2 * NB // (grid_rows * SUB)) * SUB)
    return cap, cap_top


def owner_of(row, grid_rows):
    return lax.rem(lax.div(row, NB), grid_rows)


def local_of(row, grid_rows):
    return lax.div(row, NB * grid_rows) * NB + lax.rem(row, NB)


def split(x):
    high = x.astype(jnp.bfloat16)
    return high, (x - high.astype(jnp.float32)).astype(jnp.bfloat16)


def mm(a, b):
    return jnp.dot(a, b, preferred_element_type=jnp.float32)


def gather_kernel(grid_rows, piv_ref, m_ref, rows_ref, corner_ref, owned_ref, _, line_ref, sem):
    my_row = lax.axis_index("row")
    my_col = lax.axis_index("col")
    cap = rows_ref.shape[0]
    line_ref[...] = jnp.zeros_like(line_ref)
    rows_ref[...] = jnp.zeros_like(rows_ref)

    def line_copy(row, t):
        return pltpu.make_async_copy(
            m_ref.at[pl.ds(row, 1), pl.ds(0, LANES)], line_ref.at[pl.ds(t, 1), :], sem.at[0]
        )

    def row_copy(row, slot):
        return pltpu.make_async_copy(
            m_ref.at[pl.ds(row, 1), :], rows_ref.at[pl.ds(slot, 1), :], sem.at[1]
        )

    def start(t, count):
        row = piv_ref[t]
        mine = owner_of(row, grid_rows) == my_row

        @pl.when(mine)
        def _():
            owned_ref[count] = t
            line_copy(local_of(row, grid_rows), t).start()

        @pl.when(mine & (count < cap))
        def _():
            row_copy(local_of(row, grid_rows), count).start()

        return count + mine.astype(jnp.int32)

    first = lax.fori_loop(0, NB, start, jnp.int32(0))
    count = lax.fori_loop(NB, NP, start, first)
    owned_ref[NP] = first
    owned_ref[NP + 1] = count

    def wait_line(_, carry):
        line_copy(0, 0).wait()
        return carry

    def wait_row(_, carry):
        row_copy(0, 0).wait()
        return carry

    lax.fori_loop(0, count, wait_line, 0)
    lines = line_ref[...]
    left = lax.broadcasted_iota(jnp.int32, lines.shape, 1) < NB
    corner_ref[...] = jnp.where(
        left, jnp.where(my_col == 0, lines, 0.0), jnp.where(my_col == 1, pltpu.roll(lines, NB, 1), 0.0)
    )
    lax.fori_loop(0, jnp.minimum(count, cap), wait_row, 0)


def gather_rows(matrix, pivots, cap, grid_rows):
    cols = matrix.shape[1]
    smem = pl.BlockSpec(memory_space=pltpu.SMEM)
    vmem = pl.BlockSpec(memory_space=pltpu.VMEM)
    anywhere = pl.BlockSpec(memory_space=pl.ANY)
    return pl.pallas_call(
        functools.partial(gather_kernel, grid_rows),
        out_shape=(
            jax.ShapeDtypeStruct((cap, cols), jnp.float32),
            jax.ShapeDtypeStruct((NP, LANES), jnp.float32),
            jax.ShapeDtypeStruct((NP + 2,), jnp.int32),
            jax.ShapeDtypeStruct((NP, cols), jnp.float32),
        ),
        in_specs=[smem, anywhere],
        out_specs=(vmem, vmem, smem, anywhere),
        scratch_shapes=[pltpu.VMEM((NP, LANES), jnp.float32), pltpu.SemaphoreType.DMA((2,))],
        compiler_params=pltpu.CompilerParams(vmem_limit_bytes=16 * MIB),
        name="gather_rows",
    )(pivots, matrix)


def pack_kernel(top_ref, bottom_ref, _, out_ref):
    lane = lax.broadcasted_iota(jnp.int32, out_ref.shape, 1)
    out_ref[...] = jnp.where(lane < NB, top_ref[...], pltpu.roll(bottom_ref[...], NB, 1))


def pack_panel(matrix, after, steps):
    half = matrix.shape[0] // 2
    size = half // steps
    return pl.pallas_call(
        pack_kernel,
        out_shape=jax.ShapeDtypeStruct((half, LANES), jnp.float32),
        grid=(steps,),
        in_specs=[
            pl.BlockSpec((size, LANES), lambda i: (i, 0)),
            pl.BlockSpec((size, LANES), lambda i: (i + steps, 0)),
            pl.BlockSpec(memory_space=pl.ANY),
        ],
        out_specs=pl.BlockSpec((size, LANES), lambda i: (i, 0)),
        compiler_params=pltpu.CompilerParams(vmem_limit_bytes=16 * MIB),
        name="pack_panel",
    )(matrix, matrix, after)


GROUP = 4


def eliminate_in_place(work, lane, sub):
    count = len(work)
    work = list(work)
    shape = work[0].shape
    for first in range(0, NP, GROUP):
        block, inner = divmod(first, SUB)
        below = list(range(block, count))
        cols = [
            {i: jnp.broadcast_to(work[i][:, first + j : first + j + 1], shape) for i in below}
            for j in range(GROUP)
        ]
        rows = [
            jnp.broadcast_to(work[block][inner + j : inner + j + 1, :], shape)
            for j in range(GROUP)
        ]
        spots = [
            [jnp.broadcast_to(cols[j][block][inner + i : inner + i + 1, :], shape) for j in range(GROUP)]
            for i in range(GROUP)
        ]
        scaled = []
        for j in range(GROUP):
            weight = 1.0 / spots[j][j]
            at_j = lane == first + j
            line = jnp.where(at_j, 1.0, rows[j]) * weight
            factor = {l: spots[j][l] * weight for l in range(j + 1, GROUP)}
            for i in range(j + 1, GROUP):
                rows[i] = jnp.where(at_j, 0.0, rows[i]) - spots[i][j] * line
                for l in range(j + 1, GROUP):
                    spots[i][l] = spots[i][l] - spots[i][j] * factor[l]
            for l in range(j + 1, GROUP):
                for i in below:
                    cols[l][i] = cols[l][i] - cols[j][i] * factor[l]
            later = (lane > first + j) & (lane < first + GROUP)
            scaled.append(jnp.where(later, 0.0, line))
        in_group = (lane >= first) & (lane < first + GROUP)
        for i in below:
            updated = jnp.where(in_group, 0.0, work[i])
            for j in range(GROUP):
                updated = updated - cols[j][i] * scaled[j]
            if i == block:
                updated = jnp.where(sub < inner, work[i], updated)
                for j in range(GROUP):
                    updated = jnp.where(sub == inner + j, rows[j], updated)
            work[i] = updated
    return work


def corner_kernel(corner_ref, order_ref, lu_ref, linv_ref, weights_ref):
    my_col = lax.axis_index("col")
    odd = lax.rem(my_col, 2) == 1
    a = corner_ref[...]
    a_t = a.T
    lane = lax.broadcasted_iota(jnp.int32, (SUB, LANES), 1)
    sub = lax.broadcasted_iota(jnp.int32, (SUB, LANES), 0)
    blocks = range(0, NP, SUB)
    first = eliminate_in_place([a[i : i + SUB] for i in blocks], lane, sub)
    second = eliminate_in_place([a_t[i : i + SUB] for i in blocks], lane, sub)
    w1 = jnp.concatenate(first, axis=0)
    w2 = jnp.concatenate(second, axis=0)
    row = lax.broadcasted_iota(jnp.int32, (NP, NP), 0)
    col = lax.broadcasted_iota(jnp.int32, (NP, NP), 1)
    inverse_d = 1.0 / jnp.sum(jnp.where(row == col, w1, 0.0), axis=0, keepdims=True)
    order = order_ref[...]
    linv = split(jnp.where(row > col, w1, jnp.where(row == col, 1.0, 0.0)))
    linv_ref[...] = jnp.concatenate([mm(x, order).astype(jnp.bfloat16) for x in linv], axis=1)
    w2_t = w2.T
    lu = jnp.where(row <= col, w1, w2_t * inverse_d)
    lu_ref[...] = jnp.where(my_col == 1, pltpu.roll(lu, NB, 1), lu)
    uinv = jnp.where(row < col, w2_t, jnp.where(row == col, 1.0, 0.0)) * inverse_d
    mine = jnp.where(odd, uinv[NB:], uinv[:NB])
    other = jnp.where(odd, uinv[:NB], uinv[NB:])
    zero = jnp.zeros_like(mine)
    weights_ref[0] = jnp.concatenate([mine, zero, other, zero], axis=0)
    weights_ref[1] = jnp.concatenate([zero, mine, zero, other], axis=0)


def factor_corner(corner, order):
    vmem = pl.BlockSpec(memory_space=pltpu.VMEM)
    return pl.pallas_call(
        corner_kernel,
        out_shape=(
            jax.ShapeDtypeStruct((NP, NP), jnp.float32),
            jax.ShapeDtypeStruct((NP, 2 * order.shape[1]), jnp.bfloat16),
            jax.ShapeDtypeStruct((2, 2 * NP, NP), jnp.float32),
        ),
        in_specs=[vmem, vmem],
        out_specs=(vmem, vmem, vmem),
        compiler_params=pltpu.CompilerParams(vmem_limit_bytes=24 * MIB),
        name="factor_corner",
    )(corner, order)


def upper_kernel(over_ref, rows_ref, all_ref, linv_ref, lu_ref, upper_ref, top_ref, a_ref, sem):
    my_row = lax.axis_index("row")
    my_col = lax.axis_index("col")
    count, cols = rows_ref.shape
    width = min(cols, 512)

    def solve(source_ref, depth):
        high_part = linv_ref[:, :depth]
        both = jnp.concatenate([high_part, linv_ref[:, count : count + depth]], axis=1)
        for start in range(0, cols, width):
            span = slice(start, start + width)
            high, low = split(source_ref[:, span])
            a_ref[:, span] = mm(both, jnp.concatenate([high, high], axis=0)) + mm(high_part, low)

    @pl.when(over_ref[0] == 0)
    def _():
        solve(rows_ref, count)

    @pl.when(over_ref[0] != 0)
    def _():
        copy = pltpu.make_async_copy(all_ref, a_ref, sem)
        copy.start()
        copy.wait()
        solve(a_ref, NP)

    @pl.when(my_row == 0)
    def _():
        top_ref[...] = a_ref[:NB]

    @pl.when(my_row != 0)
    def _():
        top_ref[...] = a_ref[NB:]

    @pl.when(my_col < 2)
    def _():
        lane = lax.broadcasted_iota(jnp.int32, (NP, LANES), 1)
        row = lax.broadcasted_iota(jnp.int32, (NP, LANES), 0)
        lu_part = jnp.where(my_row == 0, lu_ref[:NB], lu_ref[NB:])
        top_ref[:, :LANES] = jnp.where(lane[:NB] < NB, lu_part, top_ref[:, :LANES])
        unit = jnp.where(row == lane + my_col * NB, -1.0, 0.0)
        a_ref[:, :LANES] = jnp.where(lane < NB, unit, a_ref[:, :LANES])

    high, low = split(a_ref[...])
    upper_ref[:NP] = high
    upper_ref[NP : 2 * NP] = high
    upper_ref[2 * NP :] = low


def upper_rows_of(rows, everything, linv, lu, over):
    cols = rows.shape[1]
    smem = pl.BlockSpec(memory_space=pltpu.SMEM)
    vmem = pl.BlockSpec(memory_space=pltpu.VMEM)
    return pl.pallas_call(
        upper_kernel,
        out_shape=(
            jax.ShapeDtypeStruct((3 * NP, cols), jnp.bfloat16),
            jax.ShapeDtypeStruct((NB, cols), jnp.float32),
        ),
        in_specs=[smem, vmem, pl.BlockSpec(memory_space=pl.ANY), vmem, vmem],
        out_specs=(vmem, vmem),
        scratch_shapes=[pltpu.VMEM((NP, cols), jnp.float32), pltpu.SemaphoreType.DMA(())],
        compiler_params=pltpu.CompilerParams(vmem_limit_bytes=32 * MIB),
        name="upper_rows",
    )(over, rows, everything, linv, lu)


def lower_of(own, other, weights):
    p_high, p_low = split(jnp.concatenate([own, other], axis=1))
    w_high, w_low = split(weights)
    lower = mm(p_high, w_high) + (mm(p_high, w_low) + mm(p_low, w_high))
    high, low = split(lower)
    return jnp.concatenate([high, low, high], axis=1)


def update_rows(a_ref, lower, upper_ref, out_ref, is_panel):
    rows, cols = out_ref.shape
    width = min(cols, 256)
    lane = lax.broadcasted_iota(jnp.int32, (rows, width), 1)
    for start in range(0, cols, width):
        span = slice(start, start + width)
        a = a_ref[:, span]
        if start == 0:
            a = jnp.where((lane < NB) & is_panel, 0.0, a)
        out_ref[:, span] = a - mm(lower, upper_ref[:, span])


def moved_kernel(grid_rows, cap_top, piv_ref, m_ref, own_ref, other_ref, weights_ref, upper_ref, out_ref, *refs):
    packed_refs = refs[: grid_rows - 1]
    count_ref = refs[grid_rows - 1]
    my_row = lax.axis_index("row")
    lower = lower_of(own_ref[...], other_ref[...], weights_ref[0])
    update_rows(m_ref, lower, upper_ref, out_ref, lax.axis_index("col") < 2)
    for r in range(grid_rows):
        count_ref[r] = 0

    @pl.when(my_row < 2)
    def _():
        def place(k, carry):
            owner = owner_of(piv_ref[my_row * NB + k], grid_rows)
            slot = count_ref[owner]
            count_ref[owner] = slot + 1
            ahead = lax.rem(owner - my_row + grid_rows, grid_rows)
            for s in range(1, grid_rows):

                @pl.when((ahead == s) & (slot < cap_top))
                def _(s=s):
                    packed_refs[s - 1][pl.ds(slot, 1), :] = out_ref[pl.ds(k, 1), :]

            return carry

        lax.fori_loop(0, NB, place, 0)


def moved_rows(matrix, own, other, weights, upper, pivots, cap_top, grid_rows):
    cols = matrix.shape[1]
    smem = pl.BlockSpec(memory_space=pltpu.SMEM)
    vmem = pl.BlockSpec(memory_space=pltpu.VMEM)
    head = lambda width: pl.BlockSpec((NB, width), lambda i: (0, 0))
    return pl.pallas_call(
        functools.partial(moved_kernel, grid_rows, cap_top),
        out_shape=(jax.ShapeDtypeStruct((NB, cols), jnp.float32),)
        + (jax.ShapeDtypeStruct((cap_top, cols), jnp.float32),) * (grid_rows - 1),
        grid=(1,),
        in_specs=[smem, head(cols), head(LANES), head(LANES), vmem, vmem],
        out_specs=(head(cols),)
        + (pl.BlockSpec((cap_top, cols), lambda i: (0, 0)),) * (grid_rows - 1),
        scratch_shapes=[pltpu.SMEM((grid_rows,), jnp.int32)],
        compiler_params=pltpu.CompilerParams(vmem_limit_bytes=32 * MIB),
        name="moved_rows",
    )(pivots, matrix, own, other, weights, upper)


def trailing_kernel(m_ref, own_ref, other_ref, weights_ref, upper_ref, out_ref, lower_ref):
    step = pl.program_id(0)
    rows = m_ref.shape[0]
    half = own_ref.shape[0] // rows

    def prepare(block):
        here = pl.ds(pl.multiple_of(lax.rem(block, half) * rows, rows), rows)
        lower_ref[lax.rem(block, 2)] = lower_of(
            own_ref[here, :], other_ref[here, :], weights_ref[lax.div(block, half)]
        )

    @pl.when(step == 0)
    def _():
        prepare(step)

    update_rows(
        m_ref, lower_ref[lax.rem(step, 2)], upper_ref, out_ref, lax.axis_index("col") < 2
    )
    prepare(jnp.minimum(step + 1, 2 * half - 1))


def trailing(matrix, own, other, weights, upper):
    rows, cols = matrix.shape
    size = min(512, rows // 2)
    vmem = pl.BlockSpec(memory_space=pltpu.VMEM)
    return pl.pallas_call(
        trailing_kernel,
        out_shape=jax.ShapeDtypeStruct((rows, cols), jnp.float32),
        grid=(rows // size,),
        in_specs=[pl.BlockSpec((size, cols), lambda i: (i, 0))] + [vmem] * 4,
        out_specs=pl.BlockSpec((size, cols), lambda i: (i, 0)),
        scratch_shapes=[pltpu.VMEM((2, size, 3 * NP), jnp.bfloat16)],
        compiler_params=pltpu.CompilerParams(vmem_limit_bytes=40 * MIB),
        cost_estimate=pl.CostEstimate(
            flops=6 * rows * cols * NP, bytes_accessed=8 * rows * cols, transcendentals=0
        ),
        name="trailing",
    )(matrix, own, other, weights, upper)


def place_kernel(grid_rows, over_ref, piv_ref, owned_ref, *refs):
    moved_refs = refs[:grid_rows]
    all_ref, top_ref, _, out_ref, sem = refs[grid_rows:]
    my_row = lax.axis_index("row")
    first, total = owned_ref[NP], owned_ref[NP + 1]

    @pl.when(my_row < 2)
    def _():
        pltpu.make_async_copy(top_ref, out_ref.at[pl.ds(0, NB), :], sem).start()

    def put(source_ref, source_row, t):
        to = local_of(piv_ref[t], grid_rows)
        pltpu.make_async_copy(
            source_ref.at[pl.ds(source_row, 1), :], out_ref.at[pl.ds(to, 1), :], sem
        ).start()

    def put_from(n, carry, source_ref, row_of):
        t = owned_ref[n]
        put(source_ref, row_of(n, t), t)
        return carry

    def put_all(low, high, source_ref, row_of):
        lax.fori_loop(
            low, high, functools.partial(put_from, source_ref=source_ref, row_of=row_of), 0
        )

    packed = over_ref[0] == 0
    for panel, low, high in ((0, jnp.int32(0), first), (1, first, total)):
        back = lax.rem(my_row - panel + grid_rows, grid_rows)

        @pl.when(packed & (back == 0))
        def _(panel=panel, low=low, high=high):
            put_all(low, high, moved_refs[0], lambda n, t: t - panel * NB)

        for s in range(1, grid_rows):

            @pl.when(packed & (back == s))
            def _(s=s, low=low, high=high):
                put_all(low, high, moved_refs[s], lambda n, t: n - low)

    @pl.when(~packed)
    def _():
        put_all(0, total, all_ref, lambda n, t: t)

    def wait(_, carry):
        pltpu.make_async_copy(
            moved_refs[0].at[pl.ds(0, 1), :], out_ref.at[pl.ds(0, 1), :], sem
        ).wait()
        return carry

    lax.fori_loop(0, total, wait, 0)

    @pl.when(my_row < 2)
    def _():
        pltpu.make_async_copy(top_ref, out_ref.at[pl.ds(0, NB), :], sem).wait()


def place_moved(moved, everything, top, result, pivots, owned, over, grid_rows):
    smem = pl.BlockSpec(memory_space=pltpu.SMEM)
    anywhere = pl.BlockSpec(memory_space=pl.ANY)
    return pl.pallas_call(
        functools.partial(place_kernel, grid_rows),
        out_shape=jax.ShapeDtypeStruct(result.shape, result.dtype),
        in_specs=[smem, smem, smem] + [anywhere] * (grid_rows + 3),
        out_specs=anywhere,
        input_output_aliases={grid_rows + 5: 0},
        scratch_shapes=[pltpu.SemaphoreType.DMA(())],
        compiler_params=pltpu.CompilerParams(vmem_limit_bytes=16 * MIB),
        name="place_moved",
    )(over, pivots, owned, *moved, everything, top, result)


def spread_chips(value, order, my_chip, chips):
    reached = [0]
    for bit in order:
        pairs = [(2 * c + k, 2 * (c | bit) + k) for c in reached for k in range(2)]
        arrived = lax.ppermute(value, "col", pairs)
        value = jnp.where((my_chip & bit) != 0, arrived, value)
        reached = reached + [c | bit for c in reached]
    return value


def shards(matrix, pivots):
    grid_rows = lax.axis_size("row")
    grid_cols = lax.axis_size("col")
    chips = grid_cols // 2
    assert grid_rows > 1 and chips * 2 == grid_cols and not chips & (chips - 1)
    my_row = lax.axis_index("row")
    my_chip = lax.axis_index("col") // 2
    cap, cap_top = capacities(grid_rows)
    flat = pivots.reshape(-1)
    swap = [(c, c ^ 1) for c in range(grid_cols)]
    bits = [1 << b for b in range(chips.bit_length() - 1)]

    rows, corner, owned, unwritten = gather_rows(matrix, flat, cap, grid_rows)
    all_corner = lax.psum(corner, ("row", "col"))
    all_rows = lax.all_gather(rows, "row", tiled=True)

    packed = pack_panel(matrix, corner, 2)
    quarter = packed.shape[0] // 2
    own = jnp.concatenate(
        [
            spread_chips(packed[:quarter], bits, my_chip, chips),
            spread_chips(packed[quarter:], bits[::-1], my_chip, chips),
        ],
        axis=0,
    )
    other = lax.ppermute(own, "col", swap)

    owner = owner_of(flat, grid_rows)
    number = jnp.arange(NP, dtype=jnp.int32)
    same = owner[:, None] == owner[None, :]
    rank = jnp.sum(same & (number[None, :] < number[:, None]), axis=1, dtype=jnp.int32)
    alike = same & (number[None, :] // NB == number[:, None] // NB)
    panel_count = jnp.sum(alike, axis=1, dtype=jnp.int32)
    over = (jnp.max(jnp.maximum(rank + 1 - cap, panel_count - cap_top)) > 0).astype(jnp.int32)
    position = jnp.where(over > 0, number, owner * cap + rank)
    order = position[:, None] == jnp.arange(grid_rows * cap, dtype=jnp.int32)[None, :]
    order = order.astype(jnp.bfloat16)

    def sum_rows(state):
        mine = owner == my_row
        local = jnp.where(mine, local_of(flat, grid_rows), 0)
        picked = jnp.where(mine[:, None], matrix[local], 0.0)
        return jnp.int32(0), lax.psum(picked, "row")

    everything = lax.while_loop(lambda state: state[0] > 0, sum_rows, (over, unwritten))[1]

    over_list = over.reshape(1)
    lu, linv, weights = factor_corner(all_corner, order)
    upper, top = upper_rows_of(all_rows, everything, linv, lu, over_list)
    kept, *leaving = moved_rows(matrix, own, other, weights, upper, flat, cap_top, grid_rows)
    moved = [kept]
    for s in range(1, grid_rows):
        pairs = [(c, (c + s) % grid_rows) for c in range(2)]
        moved.append(lax.ppermute(leaving[s - 1], "row", pairs))

    def sum_moved(state):
        halves = [jnp.where(my_row == c, kept, 0.0) for c in range(2)]
        return jnp.int32(0), lax.psum(jnp.concatenate(halves, axis=0), "row")

    everything = lax.while_loop(lambda state: state[0] > 0, sum_moved, (over, everything))[1]
    result = trailing(matrix, own, other, weights, upper)
    return place_moved(moved, everything, top, result, flat, owned, over_list, grid_rows)


def solution(mesh):
    placed = (P("row", "col"), P())
    return jax.shard_map(
        shards, mesh=mesh, in_specs=placed, out_specs=P("row", "col"), check_vma=False
    )
```

```python
import functools

import jax
import jax.numpy as jnp
from jax import lax
from jax.experimental import pallas as pl
from jax.experimental.pallas import tpu as pltpu
from jax.sharding import PartitionSpec as P

NB = 64
NP = 2 * NB
LANES = 128
SUB = 8
HIGHEST_PRECISION = lax.Precision.HIGHEST
MIB = 1024 * 1024


def capacities(grid_rows):
    cap = min(NP, -(-3 * NP // (2 * grid_rows * SUB)) * SUB)
    cap_top = min(NB, -(-2 * NB // (grid_rows * SUB)) * SUB)
    return cap, cap_top


def owner_of(row, grid_rows):
    return lax.rem(lax.div(row, NB), grid_rows)


def local_of(row, grid_rows):
    return lax.div(row, NB * grid_rows) * NB + lax.rem(row, NB)


def split(x):
    high = x.astype(jnp.bfloat16)
    return high, (x - high.astype(jnp.float32)).astype(jnp.bfloat16)


def mm(a, b):
    return jnp.dot(a, b, preferred_element_type=jnp.float32)


def gather_kernel(
    grid_rows, piv_ref, m_ref, _, rows_ref, corner_ref, owned_ref, *refs
):
    line_ref, head_ref, sem = refs[1:]
    my_row = lax.axis_index("row")
    my_col = lax.axis_index("col")
    cap = rows_ref.shape[0]
    head = pltpu.make_async_copy(m_ref.at[pl.ds(0, NB), pl.ds(0, LANES)], head_ref, sem.at[2])
    head.start()
    line_ref[...] = jnp.zeros_like(line_ref)
    rows_ref[...] = jnp.zeros_like(rows_ref)

    def line_copy(row, t):
        return pltpu.make_async_copy(
            m_ref.at[pl.ds(row, 1), pl.ds(0, LANES)], line_ref.at[pl.ds(t, 1), :], sem.at[0]
        )

    def row_copy(row, slot):
        return pltpu.make_async_copy(
            m_ref.at[pl.ds(row, 1), :], rows_ref.at[pl.ds(slot, 1), :], sem.at[1]
        )

    def start(t, count):
        row = piv_ref[t]
        mine = owner_of(row, grid_rows) == my_row

        @pl.when(mine)
        def _():
            owned_ref[count] = t
            line_copy(local_of(row, grid_rows), t).start()

        @pl.when(mine & (count < cap))
        def _():
            row_copy(local_of(row, grid_rows), count).start()

        return count + mine.astype(jnp.int32)

    first = lax.fori_loop(0, NB, start, jnp.int32(0))
    count = lax.fori_loop(NB, NP, start, first)
    owned_ref[NP] = first
    owned_ref[NP + 1] = count

    def wait_line(_, carry):
        line_copy(0, 0).wait()
        return carry

    def wait_row(_, carry):
        row_copy(0, 0).wait()
        return carry

    lax.fori_loop(0, count, wait_line, 0)
    head.wait()
    left = lax.broadcasted_iota(jnp.int32, (NB, LANES), 1) < NB
    corner_ref[:NB] = jnp.where(left, line_ref[:NB], pltpu.roll(line_ref[NB:], NB, 1))
    first_half = jnp.where(my_row == 0, head_ref[...], 0.0)
    second_half = jnp.where(my_row == 1, pltpu.roll(head_ref[...], NB, 1), 0.0)
    corner_ref[NB:] = jnp.where(left, first_half, second_half)
    lax.fori_loop(0, jnp.minimum(count, cap), wait_row, 0)


def gather_rows(matrix, pivots, after, cap, grid_rows):
    cols = matrix.shape[1]
    smem = pl.BlockSpec(memory_space=pltpu.SMEM)
    vmem = pl.BlockSpec(memory_space=pltpu.VMEM)
    anywhere = pl.BlockSpec(memory_space=pl.ANY)
    return pl.pallas_call(
        functools.partial(gather_kernel, grid_rows),
        out_shape=(
            jax.ShapeDtypeStruct((cap, cols), jnp.float32),
            jax.ShapeDtypeStruct((NP, LANES), jnp.float32),
            jax.ShapeDtypeStruct((NP + 2,), jnp.int32),
            jax.ShapeDtypeStruct((NP, cols), jnp.float32),
        ),
        in_specs=[smem, anywhere, anywhere],
        out_specs=(vmem, vmem, smem, anywhere),
        scratch_shapes=[
            pltpu.VMEM((NP, LANES), jnp.float32),
            pltpu.VMEM((NB, LANES), jnp.float32),
            pltpu.SemaphoreType.DMA((3,)),
        ],
        compiler_params=pltpu.CompilerParams(vmem_limit_bytes=16 * MIB),
        name="gather_rows",
    )(pivots, matrix, after)


def pack_kernel(a_ref, b_ref, c_ref, d_ref, first_ref, second_ref):
    left = lax.broadcasted_iota(jnp.int32, first_ref.shape, 1) < NB
    first_ref[...] = jnp.where(left, a_ref[...], pltpu.roll(c_ref[...], NB, 1))
    second_ref[...] = jnp.where(left, b_ref[...], pltpu.roll(d_ref[...], NB, 1))


def pack_panel(matrix):
    size = matrix.shape[0] // 4
    piece = jax.ShapeDtypeStruct((size, LANES), jnp.float32)
    return pl.pallas_call(
        pack_kernel,
        out_shape=(piece, piece),
        grid=(1,),
        in_specs=[pl.BlockSpec((size, LANES), lambda i, k=k: (k, 0)) for k in range(4)],
        out_specs=(pl.BlockSpec((size, LANES), lambda i: (0, 0)),) * 2,
        compiler_params=pltpu.CompilerParams(vmem_limit_bytes=16 * MIB),
        name="pack_panel",
    )(matrix, matrix, matrix, matrix)


def top_kernel(grid_rows, piv_ref, m_ref, _, *refs):
    out_refs = refs[:grid_rows]
    count_ref, sem = refs[grid_rows:]
    my_row = lax.axis_index("row")
    cap_top = out_refs[0].shape[0]
    for r in range(grid_rows):
        count_ref[r] = 0

    def row_copy(k, out_ref, slot):
        return pltpu.make_async_copy(m_ref.at[pl.ds(k, 1), :], out_ref.at[pl.ds(slot, 1), :], sem)

    def start(k, total):
        owner = owner_of(piv_ref[my_row * NB + k], grid_rows)
        slot = count_ref[owner]
        count_ref[owner] = slot + 1
        ahead = lax.rem(owner - my_row + grid_rows, grid_rows)
        for s in range(grid_rows):

            @pl.when((ahead == s) & (slot < cap_top))
            def _(s=s):
                row_copy(k, out_refs[s], slot).start()

        return total + (slot < cap_top).astype(jnp.int32)

    def wait(_, carry):
        row_copy(0, out_refs[0], 0).wait()
        return carry

    @pl.when(my_row < 2)
    def _():
        total = lax.fori_loop(0, NB, start, jnp.int32(0))
        lax.fori_loop(0, total, wait, 0)


def top_rows(matrix, pivots, after, cap_top, grid_rows):
    cols = matrix.shape[1]
    smem = pl.BlockSpec(memory_space=pltpu.SMEM)
    vmem = pl.BlockSpec(memory_space=pltpu.VMEM)
    anywhere = pl.BlockSpec(memory_space=pl.ANY)
    return pl.pallas_call(
        functools.partial(top_kernel, grid_rows),
        out_shape=(jax.ShapeDtypeStruct((cap_top, cols), jnp.float32),) * grid_rows,
        in_specs=[smem, anywhere, anywhere],
        out_specs=(vmem,) * grid_rows,
        scratch_shapes=[pltpu.SMEM((grid_rows,), jnp.int32), pltpu.SemaphoreType.DMA(())],
        compiler_params=pltpu.CompilerParams(vmem_limit_bytes=16 * MIB),
        name="top_rows",
    )(pivots, matrix, after)


GROUP = 4


def eliminate_in_place(work, lane, sub):
    count = len(work)
    work = list(work)
    shape = work[0].shape
    for first in range(0, NP, GROUP):
        block, inner = divmod(first, SUB)
        below = list(range(block, count))
        cols = [
            {i: jnp.broadcast_to(work[i][:, first + j : first + j + 1], shape) for i in below}
            for j in range(GROUP)
        ]
        rows = [
            jnp.broadcast_to(work[block][inner + j : inner + j + 1, :], shape)
            for j in range(GROUP)
        ]
        spots = [
            [jnp.broadcast_to(cols[j][block][inner + i : inner + i + 1, :], shape) for j in range(GROUP)]
            for i in range(GROUP)
        ]
        scaled = []
        for j in range(GROUP):
            weight = 1.0 / spots[j][j]
            at_j = lane == first + j
            line = jnp.where(at_j, 1.0, rows[j]) * weight
            factor = {l: spots[j][l] * weight for l in range(j + 1, GROUP)}
            for i in range(j + 1, GROUP):
                rows[i] = jnp.where(at_j, 0.0, rows[i]) - spots[i][j] * line
                for l in range(j + 1, GROUP):
                    spots[i][l] = spots[i][l] - spots[i][j] * factor[l]
            for l in range(j + 1, GROUP):
                for i in below:
                    cols[l][i] = cols[l][i] - cols[j][i] * factor[l]
            later = (lane > first + j) & (lane < first + GROUP)
            scaled.append(jnp.where(later, 0.0, line))
        in_group = (lane >= first) & (lane < first + GROUP)
        for i in below:
            updated = jnp.where(in_group, 0.0, work[i])
            for j in range(GROUP):
                updated = updated - cols[j][i] * scaled[j]
            if i == block:
                updated = jnp.where(sub < inner, work[i], updated)
                for j in range(GROUP):
                    updated = jnp.where(sub == inner + j, rows[j], updated)
            work[i] = updated
    return work


def square_of(even_part, odd_part):
    left = lax.broadcasted_iota(jnp.int32, (NB, LANES), 1) < NB
    upper = jnp.where(left, even_part, pltpu.roll(odd_part, NB, 1))
    lower = jnp.where(left, pltpu.roll(even_part, NB, 1), odd_part)
    return jnp.concatenate([upper, lower], axis=0)


def corner_kernel(mine_ref, other_ref, order_ref, _, lu_ref, linv_ref, weights_ref, moved_ref):
    my_col = lax.axis_index("col")
    odd = lax.rem(my_col, 2) == 1
    even_part = jnp.where(odd, other_ref[...], mine_ref[...])
    odd_part = jnp.where(odd, mine_ref[...], other_ref[...])
    a = square_of(even_part[:NB], odd_part[:NB])
    a_t = a.T
    lane = lax.broadcasted_iota(jnp.int32, (SUB, LANES), 1)
    sub = lax.broadcasted_iota(jnp.int32, (SUB, LANES), 0)
    blocks = range(0, NP, SUB)
    first = eliminate_in_place([a[i : i + SUB] for i in blocks], lane, sub)
    second = eliminate_in_place([a_t[i : i + SUB] for i in blocks], lane, sub)
    w1 = jnp.concatenate(first, axis=0)
    w2 = jnp.concatenate(second, axis=0)
    row = lax.broadcasted_iota(jnp.int32, (NP, NP), 0)
    col = lax.broadcasted_iota(jnp.int32, (NP, NP), 1)
    inverse_d = 1.0 / jnp.sum(jnp.where(row == col, w1, 0.0), axis=0, keepdims=True)
    order = order_ref[...]
    linv = split(jnp.where(row > col, w1, jnp.where(row == col, 1.0, 0.0)))
    linv_ref[...] = jnp.concatenate([mm(x, order).astype(jnp.bfloat16) for x in linv], axis=1)
    w2_t = w2.T
    lu = jnp.where(row <= col, w1, w2_t * inverse_d)
    lu_ref[...] = jnp.where(my_col == 1, pltpu.roll(lu, NB, 1), lu)
    uinv = jnp.where(row < col, w2_t, jnp.where(row == col, 1.0, 0.0)) * inverse_d
    moved_ref[...] = multipliers(square_of(even_part[NB:], odd_part[NB:]), uinv)
    mine = jnp.where(odd, uinv[NB:], uinv[:NB])
    other = jnp.where(odd, uinv[:NB], uinv[NB:])
    zero = jnp.zeros_like(mine)
    weights_ref[0] = jnp.concatenate([mine, zero, other, zero], axis=0)
    weights_ref[1] = jnp.concatenate([zero, mine, zero, other], axis=0)


def factor_corner(mine, other, order, after):
    vmem = pl.BlockSpec(memory_space=pltpu.VMEM)
    return pl.pallas_call(
        corner_kernel,
        out_shape=(
            jax.ShapeDtypeStruct((NP, NP), jnp.float32),
            jax.ShapeDtypeStruct((NP, 2 * order.shape[1]), jnp.bfloat16),
            jax.ShapeDtypeStruct((2, 2 * NP, NP), jnp.float32),
            jax.ShapeDtypeStruct((NP, 3 * NP), jnp.bfloat16),
        ),
        in_specs=[vmem, vmem, vmem, pl.BlockSpec(memory_space=pl.ANY)],
        out_specs=(vmem,) * 4,
        compiler_params=pltpu.CompilerParams(vmem_limit_bytes=24 * MIB),
        name="factor_corner",
    )(mine, other, order, after)


def upper_kernel(rows_ref, linv_ref, lu_ref, upper_ref, top_ref, a_ref):
    my_row = lax.axis_index("row")
    my_col = lax.axis_index("col")
    count, cols = rows_ref.shape
    width = min(cols, 512)
    linv_high = linv_ref[:, :count]
    linv_both = linv_ref[...]
    for start in range(0, cols, width):
        span = slice(start, start + width)
        high, low = split(rows_ref[:, span])
        a_ref[:, span] = mm(linv_both, jnp.concatenate([high, high], axis=0)) + mm(linv_high, low)

    @pl.when(my_row == 0)
    def _():
        top_ref[...] = a_ref[:NB]

    @pl.when(my_row != 0)
    def _():
        top_ref[...] = a_ref[NB:]

    @pl.when(my_col < 2)
    def _():
        lane = lax.broadcasted_iota(jnp.int32, (NP, LANES), 1)
        row = lax.broadcasted_iota(jnp.int32, (NP, LANES), 0)
        lu_part = jnp.where(my_row == 0, lu_ref[:NB], lu_ref[NB:])
        top_ref[:, :LANES] = jnp.where(lane[:NB] < NB, lu_part, top_ref[:, :LANES])
        unit = jnp.where(row == lane + my_col * NB, -1.0, 0.0)
        a_ref[:, :LANES] = jnp.where(lane < NB, unit, a_ref[:, :LANES])

    high, low = split(a_ref[...])
    upper_ref[:NP] = high
    upper_ref[NP : 2 * NP] = high
    upper_ref[2 * NP :] = low


def upper_rows_of(rows, linv, lu):
    cols = rows.shape[1]
    vmem = pl.BlockSpec(memory_space=pltpu.VMEM)
    return pl.pallas_call(
        upper_kernel,
        out_shape=(
            jax.ShapeDtypeStruct((3 * NP, cols), jnp.bfloat16),
            jax.ShapeDtypeStruct((NB, cols), jnp.float32),
        ),
        in_specs=[vmem] * 3,
        out_specs=(vmem, vmem),
        scratch_shapes=[pltpu.VMEM((NP, cols), jnp.float32)],
        compiler_params=pltpu.CompilerParams(vmem_limit_bytes=32 * MIB),
        name="upper_rows",
    )(rows, linv, lu)


def multipliers(panel, weights):
    p_high, p_low = split(panel)
    w_high, w_low = split(weights)
    lower = mm(p_high, w_high) + (mm(p_high, w_low) + mm(p_low, w_high))
    high, low = split(lower)
    return jnp.concatenate([high, low, high], axis=1)


def update_rows(a_ref, lower, upper_ref, out_ref, is_panel):
    rows, cols = out_ref.shape
    width = min(cols, 1024)
    lane = lax.broadcasted_iota(jnp.int32, (rows, LANES), 1)

    for start in range(0, cols, width):
        span = slice(start, start + width)
        a = a_ref[:, span]
        if start == 0:
            first = jnp.where((lane < NB) & is_panel, 0.0, a[:, :LANES])
            a = jnp.concatenate([first, a[:, LANES:]], axis=1)
        out_ref[:, span] = a - mm(lower, upper_ref[:, span])


def trailing_kernel(m_ref, own_ref, other_ref, weights_ref, upper_ref, out_ref, lower_ref):
    step = pl.program_id(0)
    rows = m_ref.shape[0]
    half = own_ref.shape[0] // rows

    def prepare(block):
        here = pl.ds(pl.multiple_of(lax.rem(block, half) * rows, rows), rows)
        panel = jnp.concatenate([own_ref[here, :], other_ref[here, :]], axis=1)
        lower_ref[lax.rem(block, 2)] = multipliers(panel, weights_ref[lax.div(block, half)])

    @pl.when(step == 0)
    def _():
        prepare(step)

    update_rows(
        m_ref, lower_ref[lax.rem(step, 2)], upper_ref, out_ref, lax.axis_index("col") < 2
    )
    prepare(jnp.minimum(step + 1, 2 * half - 1))


def trailing(matrix, own, other, weights, upper):
    rows, cols = matrix.shape
    size = min(512, rows // 2)
    vmem = pl.BlockSpec(memory_space=pltpu.VMEM)
    return pl.pallas_call(
        trailing_kernel,
        out_shape=jax.ShapeDtypeStruct((rows, cols), jnp.float32),
        grid=(rows // size,),
        in_specs=[pl.BlockSpec((size, cols), lambda i: (i, 0))] + [vmem] * 4,
        out_specs=pl.BlockSpec((size, cols), lambda i: (i, 0)),
        scratch_shapes=[pltpu.VMEM((2, size, 3 * NP), jnp.bfloat16)],
        compiler_params=pltpu.CompilerParams(vmem_limit_bytes=40 * MIB),
        cost_estimate=pl.CostEstimate(
            flops=6 * rows * cols * NP, bytes_accessed=8 * rows * cols, transcendentals=0
        ),
        name="trailing",
    )(matrix, own, other, weights, upper)


def place_kernel(grid_rows, over_ref, piv_ref, owned_ref, *refs):
    piece_refs = refs[:grid_rows]
    order_ref, moved_ref, upper_ref, all_ref, top_ref, _, out_ref, f_ref, sem = refs[grid_rows:]
    my_row = lax.axis_index("row")
    first, total = owned_ref[NP], owned_ref[NP + 1]
    over = over_ref[0] != 0
    cap_top = piece_refs[0].shape[0]

    @pl.when(my_row < 2)
    def _():
        pltpu.make_async_copy(top_ref, out_ref.at[pl.ds(0, NB), :], sem.at[0]).start()

    @pl.when(over)
    def _():
        copy = pltpu.make_async_copy(all_ref, f_ref.at[pl.ds(0, NP), :], sem.at[1])
        copy.start()
        copy.wait()

    @pl.when(~over)
    def _():
        for s in range(grid_rows):
            f_ref[pl.ds(s * cap_top, cap_top), :] = piece_refs[s][...]

    lower = mm(order_ref[...], moved_ref[...]).astype(jnp.bfloat16)
    update_rows(f_ref, lower, upper_ref, f_ref, lax.axis_index("col") < 2)

    def put(n, carry, base):
        t = owned_ref[n]
        slot = jnp.where(over, t, n + base)
        pltpu.make_async_copy(
            f_ref.at[pl.ds(slot, 1), :],
            out_ref.at[pl.ds(local_of(piv_ref[t], grid_rows), 1), :],
            sem.at[1],
        ).start()
        return carry

    for panel, low, high in ((0, jnp.int32(0), first), (1, first, total)):
        back = lax.rem(my_row - panel + grid_rows, grid_rows)
        lax.fori_loop(low, high, functools.partial(put, base=back * cap_top - low), 0)

    def wait(_, carry):
        pltpu.make_async_copy(
            f_ref.at[pl.ds(0, 1), :], out_ref.at[pl.ds(0, 1), :], sem.at[1]
        ).wait()
        return carry

    lax.fori_loop(0, total, wait, 0)

    @pl.when(my_row < 2)
    def _():
        pltpu.make_async_copy(top_ref, out_ref.at[pl.ds(0, NB), :], sem.at[0]).wait()


def place_moved(pieces, order, moved, upper, everything, top, result, pivots, owned, over):
    grid_rows = len(pieces)
    cols = result.shape[1]
    smem = pl.BlockSpec(memory_space=pltpu.SMEM)
    vmem = pl.BlockSpec(memory_space=pltpu.VMEM)
    anywhere = pl.BlockSpec(memory_space=pl.ANY)
    return pl.pallas_call(
        functools.partial(place_kernel, grid_rows),
        out_shape=jax.ShapeDtypeStruct(result.shape, result.dtype),
        in_specs=[smem] * 3 + [vmem] * (grid_rows + 3) + [anywhere] * 3,
        out_specs=anywhere,
        input_output_aliases={grid_rows + 8: 0},
        scratch_shapes=[
            pltpu.VMEM((order.shape[0], cols), jnp.float32),
            pltpu.SemaphoreType.DMA((2,)),
        ],
        compiler_params=pltpu.CompilerParams(vmem_limit_bytes=24 * MIB),
        name="place_moved",
    )(over, pivots, owned, *pieces, order, moved, upper, everything, top, result)


def merge_kernel(bits, arrived1, arrived2, held1, held2, _, out_ref):
    chip = lax.div(lax.axis_index("col"), 2)
    size = held1.shape[0]
    for k, (bit, arrived, held) in enumerate(zip(bits, (arrived1, arrived2), (held1, held2))):
        here = pl.ds(k * size, size)
        came = (chip & bit) != 0

        @pl.when(came)
        def _(arrived=arrived, here=here):
            out_ref[here, :] = arrived[...]

        @pl.when(~came)
        def _(held=held, here=here):
            out_ref[here, :] = held[...]


def merge(bits, arrived, held, after):
    size = held[0].shape[0]
    vmem = pl.BlockSpec(memory_space=pltpu.VMEM)
    return pl.pallas_call(
        functools.partial(merge_kernel, bits),
        out_shape=jax.ShapeDtypeStruct((2 * size, LANES), jnp.float32),
        in_specs=[vmem] * 4 + [pl.BlockSpec(memory_space=pl.ANY)],
        out_specs=vmem,
        compiler_params=pltpu.CompilerParams(vmem_limit_bytes=16 * MIB),
        name="merge",
    )(*arrived, *held, after)


def spread_round(value, bit, reached):
    pairs = [(2 * c + k, 2 * (c | bit) + k) for c in reached for k in range(2)]
    return lax.ppermute(value, "col", pairs)


def shards(matrix, pivots):
    grid_rows = lax.axis_size("row")
    grid_cols = lax.axis_size("col")
    chips = grid_cols // 2
    assert grid_rows > 1 and chips * 2 == grid_cols and not chips & (chips - 1)
    my_row = lax.axis_index("row")
    my_chip = lax.axis_index("col") // 2
    cap, cap_top = capacities(grid_rows)
    flat = pivots.reshape(-1)
    swap = [(c, c ^ 1) for c in range(grid_cols)]
    bits = [1 << b for b in range(chips.bit_length() - 1)]

    halves = pack_panel(matrix)
    rows, corner, owned, unwritten = gather_rows(matrix, flat, halves[0], cap, grid_rows)
    all_rows = lax.all_gather(rows, "row", tiled=True)

    shifts = [[(r, (r + s) % grid_rows) for r in range(grid_rows)] for s in range(1, grid_rows)]
    corner = corner + sum(lax.ppermute(corner, "row", shift) for shift in shifts)
    corner = jnp.where(my_chip == 0, corner, 0.0) + sum(
        lax.ppermute(corner, "col", [(0, 2 * chip), (1, 2 * chip + 1)]) for chip in range(1, chips)
    )
    corner_other = lax.ppermute(corner, "col", swap)

    owner = owner_of(flat, grid_rows)
    number = jnp.arange(NP, dtype=jnp.int32)
    panel = number // NB
    same = owner[:, None] == owner[None, :]
    alike = same & (panel[None, :] == panel[:, None])
    before = number[None, :] < number[:, None]
    rank = jnp.sum(same & before, axis=1, dtype=jnp.int32)
    panel_rank = jnp.sum(alike & before, axis=1, dtype=jnp.int32)
    over = jnp.max(jnp.maximum(rank - cap, panel_rank - cap_top)) >= 0
    position = jnp.where(over, number, owner * cap + rank)
    order = position[:, None] == jnp.arange(grid_rows * cap, dtype=jnp.int32)[None, :]
    order = order.astype(jnp.bfloat16)
    back = (my_row - panel + grid_rows) % grid_rows
    slot = jnp.where(over, number, back * cap_top + panel_rank)
    slots = jnp.arange(grid_rows * cap_top, dtype=jnp.int32)
    order_top = (slot[None, :] == slots[:, None]) & (owner == my_row)[None, :]
    order_top = order_top.astype(jnp.bfloat16)
    over = over.astype(jnp.int32)
    over_list = over.reshape(1)

    quarter = halves[0].shape[0]
    held = halves
    reached = ([0], [0])
    for step, both in enumerate(zip(bits, bits[::-1])):
        arrived = [spread_round(v, bit, r) for v, bit, r in zip(held, both, reached)]
        reached = [r + [c | bit for c in r] for bit, r in zip(both, reached)]
        if step + 1 == len(bits):
            lu, linv, weights, moved = factor_corner(corner, corner_other, order, held[0])
        own = merge(both, arrived, held, corner if step + 1 < len(bits) else lu)
        held = (own[:quarter], own[quarter:])
    other = lax.ppermute(own, "col", swap)

    tops = top_rows(matrix, flat, lu, cap_top, grid_rows)
    pieces = [tops[0]]
    for s in range(1, grid_rows):
        pairs = [(c, (c + s) % grid_rows) for c in range(2)]
        pieces.append(lax.ppermute(tops[s], "row", pairs))
    def sum_rows(state):
        mine = owner == my_row
        local = jnp.where(mine, local_of(flat, grid_rows), 0)
        picked = jnp.where(mine[:, None], matrix[local], 0.0)
        tops = jnp.where((panel == my_row)[:, None], matrix[number % NB], 0.0)
        picked, tops = lax.psum((picked, tops), "row")
        return jnp.int32(0), jnp.zeros_like(state[1]).at[:NP].set(picked), tops

    _, all_rows, summed_tops = lax.while_loop(
        lambda state: state[0] > 0, sum_rows, (over, all_rows, unwritten)
    )

    upper, top = upper_rows_of(all_rows, linv, lu)
    result = trailing(matrix, own, other, weights, upper)
    return place_moved(
        pieces, order_top, moved, upper, summed_tops, top, result, flat, owned, over_list
    )


def solution(mesh):
    placed = (P("row", "col"), P())
    return jax.shard_map(
        shards, mesh=mesh, in_specs=placed, out_specs=P("row", "col"), check_vma=False
    )
```

```python
import functools

import jax
import jax.numpy as jnp
from jax import lax
from jax.experimental import pallas as pl
from jax.experimental.pallas import tpu as pltpu
from jax.sharding import PartitionSpec as P

NB = 64
NP = 2 * NB
LANES = 128
SUB = 8
HIGHEST_PRECISION = lax.Precision.HIGHEST
MIB = 1024 * 1024


def capacities(grid_rows):
    cap = min(NP, -(-3 * NP // (2 * grid_rows * SUB)) * SUB)
    cap_top = min(NB, -(-2 * NB // (grid_rows * SUB)) * SUB)
    return cap, cap_top


def owner_of(row, grid_rows):
    return lax.rem(lax.div(row, NB), grid_rows)


def local_of(row, grid_rows):
    return lax.div(row, NB * grid_rows) * NB + lax.rem(row, NB)


def split(x):
    high = x.astype(jnp.bfloat16)
    return high, (x - high.astype(jnp.float32)).astype(jnp.bfloat16)


def mm(a, b):
    return jnp.dot(a, b, preferred_element_type=jnp.float32)


def gather_kernel(
    grid_rows, piv_ref, m_ref, _, rows_ref, corner_ref, owned_ref, *refs
):
    line_ref, head_ref, sem = refs[1:]
    my_row = lax.axis_index("row")
    my_col = lax.axis_index("col")
    cap = rows_ref.shape[0]
    head = pltpu.make_async_copy(m_ref.at[pl.ds(0, NB), pl.ds(0, LANES)], head_ref, sem.at[2])
    head.start()
    line_ref[...] = jnp.zeros_like(line_ref)
    rows_ref[...] = jnp.zeros_like(rows_ref)

    def line_copy(row, t):
        return pltpu.make_async_copy(
            m_ref.at[pl.ds(row, 1), pl.ds(0, LANES)], line_ref.at[pl.ds(t, 1), :], sem.at[0]
        )

    def row_copy(row, slot):
        return pltpu.make_async_copy(
            m_ref.at[pl.ds(row, 1), :], rows_ref.at[pl.ds(slot, 1), :], sem.at[1]
        )

    def start(t, count):
        row = piv_ref[t]
        mine = owner_of(row, grid_rows) == my_row

        @pl.when(mine)
        def _():
            owned_ref[count] = t
            line_copy(local_of(row, grid_rows), t).start()

        @pl.when(mine & (count < cap))
        def _():
            row_copy(local_of(row, grid_rows), count).start()

        return count + mine.astype(jnp.int32)

    first = lax.fori_loop(0, NB, start, jnp.int32(0))
    count = lax.fori_loop(NB, NP, start, first)
    owned_ref[NP] = first
    owned_ref[NP + 1] = count

    def wait_line(_, carry):
        line_copy(0, 0).wait()
        return carry

    def wait_row(_, carry):
        row_copy(0, 0).wait()
        return carry

    lax.fori_loop(0, count, wait_line, 0)
    head.wait()
    left = lax.broadcasted_iota(jnp.int32, (NB, LANES), 1) < NB
    corner_ref[:NB] = jnp.where(left, line_ref[:NB], pltpu.roll(line_ref[NB:], NB, 1))
    first_half = jnp.where(my_row == 0, head_ref[...], 0.0)
    second_half = jnp.where(my_row == 1, pltpu.roll(head_ref[...], NB, 1), 0.0)
    corner_ref[NB:] = jnp.where(left, first_half, second_half)
    lax.fori_loop(0, jnp.minimum(count, cap), wait_row, 0)


def gather_rows(matrix, pivots, after, cap, grid_rows):
    cols = matrix.shape[1]
    smem = pl.BlockSpec(memory_space=pltpu.SMEM)
    vmem = pl.BlockSpec(memory_space=pltpu.VMEM)
    anywhere = pl.BlockSpec(memory_space=pl.ANY)
    return pl.pallas_call(
        functools.partial(gather_kernel, grid_rows),
        out_shape=(
            jax.ShapeDtypeStruct((cap, cols), jnp.float32),
            jax.ShapeDtypeStruct((NP, LANES), jnp.float32),
            jax.ShapeDtypeStruct((NP + 2,), jnp.int32),
            jax.ShapeDtypeStruct((NP, cols), jnp.float32),
        ),
        in_specs=[smem, pl.BlockSpec(memory_space=pltpu.HBM), anywhere],
        out_specs=(vmem, vmem, smem, anywhere),
        scratch_shapes=[
            pltpu.VMEM((NP, LANES), jnp.float32),
            pltpu.VMEM((NB, LANES), jnp.float32),
            pltpu.SemaphoreType.DMA((3,)),
        ],
        compiler_params=pltpu.CompilerParams(vmem_limit_bytes=16 * MIB),
        name="gather_rows",
    )(pivots, matrix, after)


def pack_kernel(a_ref, b_ref, c_ref, d_ref, first_ref, second_ref):
    left = lax.broadcasted_iota(jnp.int32, first_ref.shape, 1) < NB
    first_ref[...] = jnp.where(left, a_ref[...], pltpu.roll(c_ref[...], NB, 1))
    second_ref[...] = jnp.where(left, b_ref[...], pltpu.roll(d_ref[...], NB, 1))


def pack_panel(matrix):
    size = matrix.shape[0] // 4
    piece = jax.ShapeDtypeStruct((size, LANES), jnp.float32)
    return pl.pallas_call(
        pack_kernel,
        out_shape=(piece, piece),
        grid=(1,),
        in_specs=[pl.BlockSpec((size, LANES), lambda i, k=k: (k, 0)) for k in range(4)],
        out_specs=(pl.BlockSpec((size, LANES), lambda i: (0, 0)),) * 2,
        compiler_params=pltpu.CompilerParams(vmem_limit_bytes=16 * MIB),
        name="pack_panel",
    )(matrix, matrix, matrix, matrix)


def top_kernel(grid_rows, piv_ref, m_ref, _, *refs):
    out_refs = refs[:grid_rows]
    count_ref, sem = refs[grid_rows:]
    my_row = lax.axis_index("row")
    cap_top = out_refs[0].shape[0]
    for r in range(grid_rows):
        count_ref[r] = 0

    def row_copy(k, out_ref, slot):
        return pltpu.make_async_copy(m_ref.at[pl.ds(k, 1), :], out_ref.at[pl.ds(slot, 1), :], sem)

    def start(k, total):
        owner = owner_of(piv_ref[my_row * NB + k], grid_rows)
        slot = count_ref[owner]
        count_ref[owner] = slot + 1
        ahead = lax.rem(owner - my_row + grid_rows, grid_rows)
        for s in range(grid_rows):

            @pl.when((ahead == s) & (slot < cap_top))
            def _(s=s):
                row_copy(k, out_refs[s], slot).start()

        return total + (slot < cap_top).astype(jnp.int32)

    def wait(_, carry):
        row_copy(0, out_refs[0], 0).wait()
        return carry

    @pl.when(my_row < 2)
    def _():
        total = lax.fori_loop(0, NB, start, jnp.int32(0))
        lax.fori_loop(0, total, wait, 0)


def top_rows(matrix, pivots, after, cap_top, grid_rows):
    cols = matrix.shape[1]
    smem = pl.BlockSpec(memory_space=pltpu.SMEM)
    vmem = pl.BlockSpec(memory_space=pltpu.VMEM)
    anywhere = pl.BlockSpec(memory_space=pl.ANY)
    return pl.pallas_call(
        functools.partial(top_kernel, grid_rows),
        out_shape=(jax.ShapeDtypeStruct((cap_top, cols), jnp.float32),) * grid_rows,
        in_specs=[smem, pl.BlockSpec(memory_space=pltpu.HBM), anywhere],
        out_specs=(vmem,) * grid_rows,
        scratch_shapes=[pltpu.SMEM((grid_rows,), jnp.int32), pltpu.SemaphoreType.DMA(())],
        compiler_params=pltpu.CompilerParams(vmem_limit_bytes=16 * MIB),
        name="top_rows",
    )(pivots, matrix, after)


GROUP = 4


def eliminate_in_place(work, lane, sub):
    count = len(work)
    work = list(work)
    shape = work[0].shape
    for first in range(0, NP, GROUP):
        block, inner = divmod(first, SUB)
        below = list(range(block, count))
        cols = [
            {i: jnp.broadcast_to(work[i][:, first + j : first + j + 1], shape) for i in below}
            for j in range(GROUP)
        ]
        rows = [
            jnp.broadcast_to(work[block][inner + j : inner + j + 1, :], shape)
            for j in range(GROUP)
        ]
        spots = [
            [jnp.broadcast_to(cols[j][block][inner + i : inner + i + 1, :], shape) for j in range(GROUP)]
            for i in range(GROUP)
        ]
        scaled = []
        for j in range(GROUP):
            weight = 1.0 / spots[j][j]
            at_j = lane == first + j
            line = jnp.where(at_j, 1.0, rows[j]) * weight
            factor = {l: spots[j][l] * weight for l in range(j + 1, GROUP)}
            for i in range(j + 1, GROUP):
                rows[i] = jnp.where(at_j, 0.0, rows[i]) - spots[i][j] * line
                for l in range(j + 1, GROUP):
                    spots[i][l] = spots[i][l] - spots[i][j] * factor[l]
            for l in range(j + 1, GROUP):
                for i in below:
                    cols[l][i] = cols[l][i] - cols[j][i] * factor[l]
            later = (lane > first + j) & (lane < first + GROUP)
            scaled.append(jnp.where(later, 0.0, line))
        in_group = (lane >= first) & (lane < first + GROUP)
        for i in below:
            updated = jnp.where(in_group, 0.0, work[i])
            for j in range(GROUP):
                updated = updated - cols[j][i] * scaled[j]
            if i == block:
                updated = jnp.where(sub < inner, work[i], updated)
                for j in range(GROUP):
                    updated = jnp.where(sub == inner + j, rows[j], updated)
            work[i] = updated
    return work


def square_of(even_part, odd_part):
    left = lax.broadcasted_iota(jnp.int32, (NB, LANES), 1) < NB
    upper = jnp.where(left, even_part, pltpu.roll(odd_part, NB, 1))
    lower = jnp.where(left, pltpu.roll(even_part, NB, 1), odd_part)
    return jnp.concatenate([upper, lower], axis=0)


def corner_kernel(mine_ref, other_ref, order_ref, _, lu_ref, linv_ref, weights_ref, moved_ref):
    my_col = lax.axis_index("col")
    odd = lax.rem(my_col, 2) == 1
    even_part = jnp.where(odd, other_ref[...], mine_ref[...])
    odd_part = jnp.where(odd, mine_ref[...], other_ref[...])
    a = square_of(even_part[:NB], odd_part[:NB])
    a_t = a.T
    lane = lax.broadcasted_iota(jnp.int32, (SUB, LANES), 1)
    sub = lax.broadcasted_iota(jnp.int32, (SUB, LANES), 0)
    blocks = range(0, NP, SUB)
    first = eliminate_in_place([a[i : i + SUB] for i in blocks], lane, sub)
    second = eliminate_in_place([a_t[i : i + SUB] for i in blocks], lane, sub)
    w1 = jnp.concatenate(first, axis=0)
    w2 = jnp.concatenate(second, axis=0)
    row = lax.broadcasted_iota(jnp.int32, (NP, NP), 0)
    col = lax.broadcasted_iota(jnp.int32, (NP, NP), 1)
    inverse_d = 1.0 / jnp.sum(jnp.where(row == col, w1, 0.0), axis=0, keepdims=True)
    order = order_ref[...]
    linv = split(jnp.where(row > col, w1, jnp.where(row == col, 1.0, 0.0)))
    linv_ref[...] = jnp.concatenate([mm(x, order).astype(jnp.bfloat16) for x in linv], axis=1)
    w2_t = w2.T
    lu = jnp.where(row <= col, w1, w2_t * inverse_d)
    lu_ref[...] = jnp.where(my_col == 1, pltpu.roll(lu, NB, 1), lu)
    uinv = jnp.where(row < col, w2_t, jnp.where(row == col, 1.0, 0.0)) * inverse_d
    moved_ref[...] = multipliers(square_of(even_part[NB:], odd_part[NB:]), uinv)
    mine = jnp.where(odd, uinv[NB:], uinv[:NB])
    other = jnp.where(odd, uinv[:NB], uinv[NB:])
    zero = jnp.zeros_like(mine)
    weights_ref[0] = jnp.concatenate([mine, zero, other, zero], axis=0)
    weights_ref[1] = jnp.concatenate([zero, mine, zero, other], axis=0)


def factor_corner(mine, other, order, after):
    vmem = pl.BlockSpec(memory_space=pltpu.VMEM)
    return pl.pallas_call(
        corner_kernel,
        out_shape=(
            jax.ShapeDtypeStruct((NP, NP), jnp.float32),
            jax.ShapeDtypeStruct((NP, 2 * order.shape[1]), jnp.bfloat16),
            jax.ShapeDtypeStruct((2, 2 * NP, NP), jnp.float32),
            jax.ShapeDtypeStruct((NP, 3 * NP), jnp.bfloat16),
        ),
        in_specs=[vmem, vmem, vmem, pl.BlockSpec(memory_space=pl.ANY)],
        out_specs=(vmem,) * 4,
        compiler_params=pltpu.CompilerParams(vmem_limit_bytes=24 * MIB),
        name="factor_corner",
    )(mine, other, order, after)


def upper_kernel(rows_ref, linv_ref, lu_ref, upper_ref, top_ref, a_ref):
    my_row = lax.axis_index("row")
    my_col = lax.axis_index("col")
    count, cols = rows_ref.shape
    width = min(cols, 512)
    linv_high = linv_ref[:, :count]
    linv_both = linv_ref[...]
    for start in range(0, cols, width):
        span = slice(start, start + width)
        high, low = split(rows_ref[:, span])
        a_ref[:, span] = mm(linv_both, jnp.concatenate([high, high], axis=0)) + mm(linv_high, low)

    @pl.when(my_row == 0)
    def _():
        top_ref[...] = a_ref[:NB]

    @pl.when(my_row != 0)
    def _():
        top_ref[...] = a_ref[NB:]

    @pl.when(my_col < 2)
    def _():
        lane = lax.broadcasted_iota(jnp.int32, (NP, LANES), 1)
        row = lax.broadcasted_iota(jnp.int32, (NP, LANES), 0)
        lu_part = jnp.where(my_row == 0, lu_ref[:NB], lu_ref[NB:])
        top_ref[:, :LANES] = jnp.where(lane[:NB] < NB, lu_part, top_ref[:, :LANES])
        unit = jnp.where(row == lane + my_col * NB, -1.0, 0.0)
        a_ref[:, :LANES] = jnp.where(lane < NB, unit, a_ref[:, :LANES])

    high, low = split(a_ref[...])
    upper_ref[:NP] = high
    upper_ref[NP : 2 * NP] = high
    upper_ref[2 * NP :] = low


def upper_rows_of(rows, linv, lu):
    cols = rows.shape[1]
    vmem = pl.BlockSpec(memory_space=pltpu.VMEM)
    return pl.pallas_call(
        upper_kernel,
        out_shape=(
            jax.ShapeDtypeStruct((3 * NP, cols), jnp.bfloat16),
            jax.ShapeDtypeStruct((NB, cols), jnp.float32),
        ),
        in_specs=[vmem] * 3,
        out_specs=(vmem, vmem),
        scratch_shapes=[pltpu.VMEM((NP, cols), jnp.float32)],
        compiler_params=pltpu.CompilerParams(vmem_limit_bytes=32 * MIB),
        name="upper_rows",
    )(rows, linv, lu)


def multipliers(panel, weights):
    p_high, p_low = split(panel)
    w_high, w_low = split(weights)
    lower = mm(p_high, w_high) + (mm(p_high, w_low) + mm(p_low, w_high))
    high, low = split(lower)
    return jnp.concatenate([high, low, high], axis=1)


def update_rows(a_ref, lower, upper_ref, out_ref, is_panel):
    rows, cols = out_ref.shape
    width = min(cols, 1024)
    lane = lax.broadcasted_iota(jnp.int32, (rows, LANES), 1)

    for start in range(0, cols, width):
        span = slice(start, start + width)
        a = a_ref[:, span]
        if start == 0:
            first = jnp.where((lane < NB) & is_panel, 0.0, a[:, :LANES])
            a = jnp.concatenate([first, a[:, LANES:]], axis=1)
        out_ref[:, span] = a - mm(lower, upper_ref[:, span])


def lower_kernel(own_ref, other_ref, weights_ref, out_ref):
    panel = jnp.concatenate([own_ref[...], other_ref[...]], axis=1)
    out_ref[...] = multipliers(panel, weights_ref[0])


def lower_rows(own, other, weights):
    half = own.shape[0]
    size = min(1024, half)
    steps = half // size
    packed = pl.BlockSpec((size, LANES), lambda i: (lax.rem(i, steps), 0))
    return pl.pallas_call(
        lower_kernel,
        out_shape=jax.ShapeDtypeStruct((2 * half, 3 * NP), jnp.bfloat16),
        grid=(2 * steps,),
        in_specs=[
            packed,
            packed,
            pl.BlockSpec((1, 2 * NP, NP), lambda i: (lax.div(i, steps), 0, 0)),
        ],
        out_specs=pl.BlockSpec((size, 3 * NP), lambda i: (i, 0)),
        compiler_params=pltpu.CompilerParams(vmem_limit_bytes=24 * MIB),
        name="lower_rows",
    )(own, other, weights)


def trailing(matrix, lower, upper, is_panel):
    column = jnp.arange(matrix.shape[1], dtype=jnp.int32)
    kept = jnp.where((is_panel & (column < NB))[None, :], 0.0, matrix)
    return kept - mm(lower, upper)


def place_kernel(grid_rows, over_ref, piv_ref, owned_ref, *refs):
    piece_refs = refs[:grid_rows]
    order_ref, moved_ref, upper_ref, all_ref, top_ref, _, out_ref, f_ref, sem = refs[grid_rows:]
    my_row = lax.axis_index("row")
    first, total = owned_ref[NP], owned_ref[NP + 1]
    over = over_ref[0] != 0
    cap_top = piece_refs[0].shape[0]

    @pl.when(my_row < 2)
    def _():
        pltpu.make_async_copy(top_ref, out_ref.at[pl.ds(0, NB), :], sem.at[0]).start()

    @pl.when(over)
    def _():
        copy = pltpu.make_async_copy(all_ref, f_ref.at[pl.ds(0, NP), :], sem.at[1])
        copy.start()
        copy.wait()

    @pl.when(~over)
    def _():
        for s in range(grid_rows):
            f_ref[pl.ds(s * cap_top, cap_top), :] = piece_refs[s][...]

    lower = mm(order_ref[...], moved_ref[...]).astype(jnp.bfloat16)
    update_rows(f_ref, lower, upper_ref, f_ref, lax.axis_index("col") < 2)

    def put(n, carry, base):
        t = owned_ref[n]
        slot = jnp.where(over, t, n + base)
        pltpu.make_async_copy(
            f_ref.at[pl.ds(slot, 1), :],
            out_ref.at[pl.ds(local_of(piv_ref[t], grid_rows), 1), :],
            sem.at[1],
        ).start()
        return carry

    for panel, low, high in ((0, jnp.int32(0), first), (1, first, total)):
        back = lax.rem(my_row - panel + grid_rows, grid_rows)
        lax.fori_loop(low, high, functools.partial(put, base=back * cap_top - low), 0)

    def wait(_, carry):
        pltpu.make_async_copy(
            f_ref.at[pl.ds(0, 1), :], out_ref.at[pl.ds(0, 1), :], sem.at[1]
        ).wait()
        return carry

    lax.fori_loop(0, total, wait, 0)

    @pl.when(my_row < 2)
    def _():
        pltpu.make_async_copy(top_ref, out_ref.at[pl.ds(0, NB), :], sem.at[0]).wait()


def place_moved(pieces, order, moved, upper, everything, top, result, pivots, owned, over):
    grid_rows = len(pieces)
    cols = result.shape[1]
    smem = pl.BlockSpec(memory_space=pltpu.SMEM)
    vmem = pl.BlockSpec(memory_space=pltpu.VMEM)
    anywhere = pl.BlockSpec(memory_space=pl.ANY)
    return pl.pallas_call(
        functools.partial(place_kernel, grid_rows),
        out_shape=jax.ShapeDtypeStruct(result.shape, result.dtype),
        in_specs=[smem] * 3 + [vmem] * (grid_rows + 3) + [anywhere] * 3,
        out_specs=anywhere,
        input_output_aliases={grid_rows + 8: 0},
        scratch_shapes=[
            pltpu.VMEM((order.shape[0], cols), jnp.float32),
            pltpu.SemaphoreType.DMA((2,)),
        ],
        compiler_params=pltpu.CompilerParams(vmem_limit_bytes=24 * MIB),
        name="place_moved",
    )(over, pivots, owned, *pieces, order, moved, upper, everything, top, result)


def merge_kernel(bits, arrived1, arrived2, held1, held2, _, out_ref):
    chip = lax.div(lax.axis_index("col"), 2)
    size = held1.shape[0]
    for k, (bit, arrived, held) in enumerate(zip(bits, (arrived1, arrived2), (held1, held2))):
        here = pl.ds(k * size, size)
        came = (chip & bit) != 0

        @pl.when(came)
        def _(arrived=arrived, here=here):
            out_ref[here, :] = arrived[...]

        @pl.when(~came)
        def _(held=held, here=here):
            out_ref[here, :] = held[...]


def merge(bits, arrived, held, after):
    size = held[0].shape[0]
    vmem = pl.BlockSpec(memory_space=pltpu.VMEM)
    return pl.pallas_call(
        functools.partial(merge_kernel, bits),
        out_shape=jax.ShapeDtypeStruct((2 * size, LANES), jnp.float32),
        in_specs=[vmem] * 4 + [pl.BlockSpec(memory_space=pl.ANY)],
        out_specs=vmem,
        compiler_params=pltpu.CompilerParams(vmem_limit_bytes=16 * MIB),
        name="merge",
    )(*arrived, *held, after)


def spread_round(value, bit, reached):
    pairs = [(2 * c + k, 2 * (c | bit) + k) for c in reached for k in range(2)]
    return lax.ppermute(value, "col", pairs)


def shards(matrix, pivots):
    grid_rows = lax.axis_size("row")
    grid_cols = lax.axis_size("col")
    chips = grid_cols // 2
    assert grid_rows > 1 and chips * 2 == grid_cols and not chips & (chips - 1)
    my_row = lax.axis_index("row")
    my_chip = lax.axis_index("col") // 2
    cap, cap_top = capacities(grid_rows)
    flat = pivots.reshape(-1)
    swap = [(c, c ^ 1) for c in range(grid_cols)]
    bits = [1 << b for b in range(chips.bit_length() - 1)]

    halves = pack_panel(matrix)
    rows, corner, owned, unwritten = gather_rows(matrix, flat, halves[0], cap, grid_rows)
    all_rows = lax.all_gather(rows, "row", tiled=True)

    shifts = [[(r, (r + s) % grid_rows) for r in range(grid_rows)] for s in range(1, grid_rows)]
    corner = corner + sum(lax.ppermute(corner, "row", shift) for shift in shifts)
    corner = jnp.where(my_chip == 0, corner, 0.0) + sum(
        lax.ppermute(corner, "col", [(0, 2 * chip), (1, 2 * chip + 1)]) for chip in range(1, chips)
    )
    corner_other = lax.ppermute(corner, "col", swap)

    owner = owner_of(flat, grid_rows)
    number = jnp.arange(NP, dtype=jnp.int32)
    panel = number // NB
    same = owner[:, None] == owner[None, :]
    alike = same & (panel[None, :] == panel[:, None])
    before = number[None, :] < number[:, None]
    rank = jnp.sum(same & before, axis=1, dtype=jnp.int32)
    panel_rank = jnp.sum(alike & before, axis=1, dtype=jnp.int32)
    over = jnp.max(jnp.maximum(rank - cap, panel_rank - cap_top)) >= 0
    position = jnp.where(over, number, owner * cap + rank)
    order = position[:, None] == jnp.arange(grid_rows * cap, dtype=jnp.int32)[None, :]
    order = order.astype(jnp.bfloat16)
    back = (my_row - panel + grid_rows) % grid_rows
    slot = jnp.where(over, number, back * cap_top + panel_rank)
    slots = jnp.arange(grid_rows * cap_top, dtype=jnp.int32)
    order_top = (slot[None, :] == slots[:, None]) & (owner == my_row)[None, :]
    order_top = order_top.astype(jnp.bfloat16)
    over = over.astype(jnp.int32)
    over_list = over.reshape(1)

    quarter = halves[0].shape[0]
    held = halves
    reached = ([0], [0])
    for step, both in enumerate(zip(bits, bits[::-1])):
        arrived = [spread_round(v, bit, r) for v, bit, r in zip(held, both, reached)]
        reached = [r + [c | bit for c in r] for bit, r in zip(both, reached)]
        if step + 1 == len(bits):
            lu, linv, weights, moved = factor_corner(corner, corner_other, order, held[0])
        own = merge(both, arrived, held, corner if step + 1 < len(bits) else lu)
        held = (own[:quarter], own[quarter:])
    other = lax.ppermute(own, "col", swap)

    tops = top_rows(matrix, flat, lu, cap_top, grid_rows)
    pieces = [tops[0]]
    for s in range(1, grid_rows):
        pairs = [(c, (c + s) % grid_rows) for c in range(2)]
        pieces.append(lax.ppermute(tops[s], "row", pairs))
    def sum_rows(state):
        mine = owner == my_row
        local = jnp.where(mine, local_of(flat, grid_rows), 0)
        picked = jnp.where(mine[:, None], matrix[local], 0.0)
        tops = jnp.where((panel == my_row)[:, None], matrix[number % NB], 0.0)
        picked, tops = lax.psum((picked, tops), "row")
        return jnp.int32(0), jnp.zeros_like(state[1]).at[:NP].set(picked), tops

    _, all_rows, summed_tops = lax.while_loop(
        lambda state: state[0] > 0, sum_rows, (over, all_rows, unwritten)
    )

    upper, top = upper_rows_of(all_rows, linv, lu)
    lower = lower_rows(own, other, weights)
    result = trailing(matrix, lower, upper, lax.axis_index("col") < 2)
    return place_moved(
        pieces, order_top, moved, upper, summed_tops, top, result, flat, owned, over_list
    )


def solution(mesh):
    placed = (P("row", "col"), P())
    return jax.shard_map(
        shards, mesh=mesh, in_specs=placed, out_specs=P("row", "col"), check_vma=False
    )
```

```python
import functools

import jax
import jax.numpy as jnp
from jax import lax
from jax.experimental import pallas as pl
from jax.experimental.pallas import tpu as pltpu
from jax.sharding import PartitionSpec as P

NB = 64
NP = 2 * NB
LANES = 128
SUB = 8
HIGHEST_PRECISION = lax.Precision.HIGHEST
MIB = 1024 * 1024


def capacities(grid_rows):
    cap = min(NP, -(-3 * NP // (2 * grid_rows * SUB)) * SUB)
    cap_top = min(NB, -(-2 * NB // (grid_rows * SUB)) * SUB)
    return cap, cap_top


def owner_of(row, grid_rows):
    return lax.rem(lax.div(row, NB), grid_rows)


def local_of(row, grid_rows):
    return lax.div(row, NB * grid_rows) * NB + lax.rem(row, NB)


def split(x):
    high = x.astype(jnp.bfloat16)
    return high, (x - high.astype(jnp.float32)).astype(jnp.bfloat16)


def mm(a, b):
    return jnp.dot(a, b, preferred_element_type=jnp.float32)


def gather_kernel(
    grid_rows, piv_ref, m_ref, _, rows_ref, corner_ref, owned_ref, *refs
):
    line_ref, head_ref, sem = refs[1:]
    my_row = lax.axis_index("row")
    my_col = lax.axis_index("col")
    cap = rows_ref.shape[0]
    head = pltpu.make_async_copy(m_ref.at[pl.ds(0, NB), pl.ds(0, LANES)], head_ref, sem.at[2])
    head.start()
    line_ref[...] = jnp.zeros_like(line_ref)
    rows_ref[...] = jnp.zeros_like(rows_ref)

    def line_copy(row, t):
        return pltpu.make_async_copy(
            m_ref.at[pl.ds(row, 1), pl.ds(0, LANES)], line_ref.at[pl.ds(t, 1), :], sem.at[0]
        )

    def row_copy(row, slot):
        return pltpu.make_async_copy(
            m_ref.at[pl.ds(row, 1), :], rows_ref.at[pl.ds(slot, 1), :], sem.at[1]
        )

    def start(t, count):
        row = piv_ref[t]
        mine = owner_of(row, grid_rows) == my_row

        @pl.when(mine)
        def _():
            owned_ref[count] = t
            line_copy(local_of(row, grid_rows), t).start()

        @pl.when(mine & (count < cap))
        def _():
            row_copy(local_of(row, grid_rows), count).start()

        return count + mine.astype(jnp.int32)

    first = lax.fori_loop(0, NB, start, jnp.int32(0))
    count = lax.fori_loop(NB, NP, start, first)
    owned_ref[NP] = first
    owned_ref[NP + 1] = count

    def wait_line(_, carry):
        line_copy(0, 0).wait()
        return carry

    def wait_row(_, carry):
        row_copy(0, 0).wait()
        return carry

    lax.fori_loop(0, count, wait_line, 0)
    head.wait()
    left = lax.broadcasted_iota(jnp.int32, (NB, LANES), 1) < NB
    corner_ref[:NB] = jnp.where(left, line_ref[:NB], pltpu.roll(line_ref[NB:], NB, 1))
    first_half = jnp.where(my_row == 0, head_ref[...], 0.0)
    second_half = jnp.where(my_row == 1, pltpu.roll(head_ref[...], NB, 1), 0.0)
    corner_ref[NB:] = jnp.where(left, first_half, second_half)
    lax.fori_loop(0, jnp.minimum(count, cap), wait_row, 0)


def gather_rows(matrix, pivots, after, cap, grid_rows):
    cols = matrix.shape[1]
    smem = pl.BlockSpec(memory_space=pltpu.SMEM)
    vmem = pl.BlockSpec(memory_space=pltpu.VMEM)
    anywhere = pl.BlockSpec(memory_space=pl.ANY)
    return pl.pallas_call(
        functools.partial(gather_kernel, grid_rows),
        out_shape=(
            jax.ShapeDtypeStruct((cap, cols), jnp.float32),
            jax.ShapeDtypeStruct((NP, LANES), jnp.float32),
            jax.ShapeDtypeStruct((NP + 2,), jnp.int32),
            jax.ShapeDtypeStruct((NP, cols), jnp.float32),
        ),
        in_specs=[smem, pl.BlockSpec(memory_space=pltpu.HBM), anywhere],
        out_specs=(vmem, vmem, smem, anywhere),
        scratch_shapes=[
            pltpu.VMEM((NP, LANES), jnp.float32),
            pltpu.VMEM((NB, LANES), jnp.float32),
            pltpu.SemaphoreType.DMA((3,)),
        ],
        compiler_params=pltpu.CompilerParams(vmem_limit_bytes=16 * MIB),
        name="gather_rows",
    )(pivots, matrix, after)


def pack_kernel(a_ref, b_ref, c_ref, d_ref, first_ref, second_ref):
    left = lax.broadcasted_iota(jnp.int32, first_ref.shape, 1) < NB
    first_ref[...] = jnp.where(left, a_ref[...], pltpu.roll(c_ref[...], NB, 1))
    second_ref[...] = jnp.where(left, b_ref[...], pltpu.roll(d_ref[...], NB, 1))


def pack_panel(matrix):
    size = matrix.shape[0] // 4
    piece = jax.ShapeDtypeStruct((size, LANES), jnp.float32)
    return pl.pallas_call(
        pack_kernel,
        out_shape=(piece, piece),
        grid=(1,),
        in_specs=[pl.BlockSpec((size, LANES), lambda i, k=k: (k, 0)) for k in range(4)],
        out_specs=(pl.BlockSpec((size, LANES), lambda i: (0, 0)),) * 2,
        compiler_params=pltpu.CompilerParams(vmem_limit_bytes=16 * MIB),
        name="pack_panel",
    )(matrix, matrix, matrix, matrix)


def top_kernel(grid_rows, piv_ref, m_ref, _, *refs):
    out_refs = refs[:grid_rows]
    count_ref, sem = refs[grid_rows:]
    my_row = lax.axis_index("row")
    cap_top = out_refs[0].shape[0]
    for r in range(grid_rows):
        count_ref[r] = 0

    def row_copy(k, out_ref, slot):
        return pltpu.make_async_copy(m_ref.at[pl.ds(k, 1), :], out_ref.at[pl.ds(slot, 1), :], sem)

    def start(k, total):
        owner = owner_of(piv_ref[my_row * NB + k], grid_rows)
        slot = count_ref[owner]
        count_ref[owner] = slot + 1
        ahead = lax.rem(owner - my_row + grid_rows, grid_rows)
        for s in range(grid_rows):

            @pl.when((ahead == s) & (slot < cap_top))
            def _(s=s):
                row_copy(k, out_refs[s], slot).start()

        return total + (slot < cap_top).astype(jnp.int32)

    def wait(_, carry):
        row_copy(0, out_refs[0], 0).wait()
        return carry

    @pl.when(my_row < 2)
    def _():
        total = lax.fori_loop(0, NB, start, jnp.int32(0))
        lax.fori_loop(0, total, wait, 0)


def top_rows(matrix, pivots, after, cap_top, grid_rows):
    cols = matrix.shape[1]
    smem = pl.BlockSpec(memory_space=pltpu.SMEM)
    vmem = pl.BlockSpec(memory_space=pltpu.VMEM)
    anywhere = pl.BlockSpec(memory_space=pl.ANY)
    return pl.pallas_call(
        functools.partial(top_kernel, grid_rows),
        out_shape=(jax.ShapeDtypeStruct((cap_top, cols), jnp.float32),) * grid_rows,
        in_specs=[smem, pl.BlockSpec(memory_space=pltpu.HBM), anywhere],
        out_specs=(vmem,) * grid_rows,
        scratch_shapes=[pltpu.SMEM((grid_rows,), jnp.int32), pltpu.SemaphoreType.DMA(())],
        compiler_params=pltpu.CompilerParams(vmem_limit_bytes=16 * MIB),
        name="top_rows",
    )(pivots, matrix, after)


GROUP = 4


def eliminate_in_place(work, lane, sub):
    count = len(work)
    work = list(work)
    shape = work[0].shape
    for first in range(0, NP, GROUP):
        block, inner = divmod(first, SUB)
        below = list(range(block, count))
        cols = [
            {i: jnp.broadcast_to(work[i][:, first + j : first + j + 1], shape) for i in below}
            for j in range(GROUP)
        ]
        rows = [
            jnp.broadcast_to(work[block][inner + j : inner + j + 1, :], shape)
            for j in range(GROUP)
        ]
        spots = [
            [jnp.broadcast_to(cols[j][block][inner + i : inner + i + 1, :], shape) for j in range(GROUP)]
            for i in range(GROUP)
        ]
        scaled = []
        for j in range(GROUP):
            weight = 1.0 / spots[j][j]
            at_j = lane == first + j
            line = jnp.where(at_j, 1.0, rows[j]) * weight
            factor = {l: spots[j][l] * weight for l in range(j + 1, GROUP)}
            for i in range(j + 1, GROUP):
                rows[i] = jnp.where(at_j, 0.0, rows[i]) - spots[i][j] * line
                for l in range(j + 1, GROUP):
                    spots[i][l] = spots[i][l] - spots[i][j] * factor[l]
            for l in range(j + 1, GROUP):
                for i in below:
                    cols[l][i] = cols[l][i] - cols[j][i] * factor[l]
            later = (lane > first + j) & (lane < first + GROUP)
            scaled.append(jnp.where(later, 0.0, line))
        in_group = (lane >= first) & (lane < first + GROUP)
        for i in below:
            updated = jnp.where(in_group, 0.0, work[i])
            for j in range(GROUP):
                updated = updated - cols[j][i] * scaled[j]
            if i == block:
                updated = jnp.where(sub < inner, work[i], updated)
                for j in range(GROUP):
                    updated = jnp.where(sub == inner + j, rows[j], updated)
            work[i] = updated
    return work


def square_of(even_part, odd_part):
    left = lax.broadcasted_iota(jnp.int32, (NB, LANES), 1) < NB
    upper = jnp.where(left, even_part, pltpu.roll(odd_part, NB, 1))
    lower = jnp.where(left, pltpu.roll(even_part, NB, 1), odd_part)
    return jnp.concatenate([upper, lower], axis=0)


def corner_kernel(mine_ref, other_ref, order_ref, _, lu_ref, linv_ref, weights_ref, moved_ref):
    my_col = lax.axis_index("col")
    odd = lax.rem(my_col, 2) == 1
    even_part = jnp.where(odd, other_ref[...], mine_ref[...])
    odd_part = jnp.where(odd, mine_ref[...], other_ref[...])
    a = square_of(even_part[:NB], odd_part[:NB])
    a_t = a.T
    lane = lax.broadcasted_iota(jnp.int32, (SUB, LANES), 1)
    sub = lax.broadcasted_iota(jnp.int32, (SUB, LANES), 0)
    blocks = range(0, NP, SUB)
    first = eliminate_in_place([a[i : i + SUB] for i in blocks], lane, sub)
    second = eliminate_in_place([a_t[i : i + SUB] for i in blocks], lane, sub)
    w1 = jnp.concatenate(first, axis=0)
    w2 = jnp.concatenate(second, axis=0)
    row = lax.broadcasted_iota(jnp.int32, (NP, NP), 0)
    col = lax.broadcasted_iota(jnp.int32, (NP, NP), 1)
    inverse_d = 1.0 / jnp.sum(jnp.where(row == col, w1, 0.0), axis=0, keepdims=True)
    order = order_ref[...]
    linv = split(jnp.where(row > col, w1, jnp.where(row == col, 1.0, 0.0)))
    linv_ref[...] = jnp.concatenate([mm(x, order).astype(jnp.bfloat16) for x in linv], axis=1)
    w2_t = w2.T
    lu = jnp.where(row <= col, w1, w2_t * inverse_d)
    lu_ref[...] = jnp.where(my_col == 1, pltpu.roll(lu, NB, 1), lu)
    uinv = jnp.where(row < col, w2_t, jnp.where(row == col, 1.0, 0.0)) * inverse_d
    moved_ref[...] = multipliers(square_of(even_part[NB:], odd_part[NB:]), uinv)
    mine = jnp.where(odd, uinv[NB:], uinv[:NB])
    other = jnp.where(odd, uinv[:NB], uinv[NB:])
    zero = jnp.zeros_like(mine)
    weights_ref[0] = jnp.concatenate([mine, zero, other, zero], axis=0)
    weights_ref[1] = jnp.concatenate([zero, mine, zero, other], axis=0)


def factor_corner(mine, other, order, after):
    vmem = pl.BlockSpec(memory_space=pltpu.VMEM)
    return pl.pallas_call(
        corner_kernel,
        out_shape=(
            jax.ShapeDtypeStruct((NP, NP), jnp.float32),
            jax.ShapeDtypeStruct((NP, 2 * order.shape[1]), jnp.bfloat16),
            jax.ShapeDtypeStruct((2, 2 * NP, NP), jnp.float32),
            jax.ShapeDtypeStruct((NP, 3 * NP), jnp.bfloat16),
        ),
        in_specs=[vmem, vmem, vmem, pl.BlockSpec(memory_space=pl.ANY)],
        out_specs=(vmem,) * 4,
        compiler_params=pltpu.CompilerParams(vmem_limit_bytes=24 * MIB),
        name="factor_corner",
    )(mine, other, order, after)


def upper_kernel(rows_ref, linv_ref, lu_ref, upper_ref, top_ref, a_ref):
    my_row = lax.axis_index("row")
    my_col = lax.axis_index("col")
    count, cols = rows_ref.shape
    width = min(cols, 512)
    linv_high = linv_ref[:, :count]
    linv_both = linv_ref[...]
    for start in range(0, cols, width):
        span = slice(start, start + width)
        high, low = split(rows_ref[:, span])
        a_ref[:, span] = mm(linv_both, jnp.concatenate([high, high], axis=0)) + mm(linv_high, low)

    @pl.when(my_row == 0)
    def _():
        top_ref[...] = a_ref[:NB]

    @pl.when(my_row != 0)
    def _():
        top_ref[...] = a_ref[NB:]

    @pl.when(my_col < 2)
    def _():
        lane = lax.broadcasted_iota(jnp.int32, (NP, LANES), 1)
        row = lax.broadcasted_iota(jnp.int32, (NP, LANES), 0)
        lu_part = jnp.where(my_row == 0, lu_ref[:NB], lu_ref[NB:])
        top_ref[:, :LANES] = jnp.where(lane[:NB] < NB, lu_part, top_ref[:, :LANES])
        unit = jnp.where(row == lane + my_col * NB, -1.0, 0.0)
        a_ref[:, :LANES] = jnp.where(lane < NB, unit, a_ref[:, :LANES])

    high, low = split(a_ref[...])
    upper_ref[:NP] = high
    upper_ref[NP : 2 * NP] = high
    upper_ref[2 * NP :] = low


def upper_rows_of(rows, linv, lu):
    cols = rows.shape[1]
    vmem = pl.BlockSpec(memory_space=pltpu.VMEM)
    return pl.pallas_call(
        upper_kernel,
        out_shape=(
            jax.ShapeDtypeStruct((3 * NP, cols), jnp.bfloat16),
            jax.ShapeDtypeStruct((NB, cols), jnp.float32),
        ),
        in_specs=[vmem] * 3,
        out_specs=(vmem, vmem),
        scratch_shapes=[pltpu.VMEM((NP, cols), jnp.float32)],
        compiler_params=pltpu.CompilerParams(vmem_limit_bytes=32 * MIB),
        name="upper_rows",
    )(rows, linv, lu)


def multipliers(panel, weights):
    p_high, p_low = split(panel)
    w_high, w_low = split(weights)
    lower = mm(p_high, w_high) + (mm(p_high, w_low) + mm(p_low, w_high))
    high, low = split(lower)
    return jnp.concatenate([high, low, high], axis=1)


def update_rows(a_ref, lower, upper_ref, out_ref, is_panel):
    rows, cols = out_ref.shape
    width = min(cols, 512)
    lane = lax.broadcasted_iota(jnp.int32, (rows, LANES), 1)

    for start in range(0, cols, width):
        span = slice(start, start + width)
        a = a_ref[:, span]
        if start == 0:
            first = jnp.where((lane < NB) & is_panel, 0.0, a[:, :LANES])
            a = jnp.concatenate([first, a[:, LANES:]], axis=1)
        out_ref[:, span] = a - mm(lower, upper_ref[:, span])


def lower_kernel(own_ref, other_ref, weights_ref, out_ref):
    panel = jnp.concatenate([own_ref[...], other_ref[...]], axis=1)
    out_ref[...] = multipliers(panel, weights_ref[0])


def lower_rows(own, other, weights):
    half = own.shape[0]
    size = min(1024, half)
    steps = half // size
    packed = pl.BlockSpec((size, LANES), lambda i: (lax.rem(i, steps), 0))
    return pl.pallas_call(
        lower_kernel,
        out_shape=jax.ShapeDtypeStruct((2 * half, 3 * NP), jnp.bfloat16),
        grid=(2 * steps,),
        in_specs=[
            packed,
            packed,
            pl.BlockSpec((1, 2 * NP, NP), lambda i: (lax.div(i, steps), 0, 0)),
        ],
        out_specs=pl.BlockSpec((size, 3 * NP), lambda i: (i, 0)),
        compiler_params=pltpu.CompilerParams(vmem_limit_bytes=24 * MIB),
        name="lower_rows",
    )(own, other, weights)


def trailing_kernel(m_ref, lower_ref, upper_ref, out_ref):
    update_rows(m_ref, lower_ref[...], upper_ref, out_ref, lax.axis_index("col") < 2)


def trailing(matrix, lower, upper):
    rows, cols = matrix.shape
    size = min(512, rows)
    block = pl.BlockSpec((size, cols), lambda i: (i, 0))
    return pl.pallas_call(
        trailing_kernel,
        out_shape=jax.ShapeDtypeStruct((rows, cols), jnp.float32),
        grid=(rows // size,),
        in_specs=[
            block,
            pl.BlockSpec((size, 3 * NP), lambda i: (i, 0)),
            pl.BlockSpec(memory_space=pltpu.VMEM),
        ],
        out_specs=block,
        compiler_params=pltpu.CompilerParams(vmem_limit_bytes=28 * MIB),
        cost_estimate=pl.CostEstimate(
            flops=6 * rows * cols * NP, bytes_accessed=8 * rows * cols, transcendentals=0
        ),
        name="trailing",
    )(matrix, lower, upper)


def place_kernel(grid_rows, over_ref, piv_ref, owned_ref, *refs):
    piece_refs = refs[:grid_rows]
    order_ref, moved_ref, upper_ref, all_ref, top_ref, _, out_ref, f_ref, sem = refs[grid_rows:]
    my_row = lax.axis_index("row")
    first, total = owned_ref[NP], owned_ref[NP + 1]
    over = over_ref[0] != 0
    cap_top = piece_refs[0].shape[0]

    @pl.when(my_row < 2)
    def _():
        pltpu.make_async_copy(top_ref, out_ref.at[pl.ds(0, NB), :], sem.at[0]).start()

    @pl.when(over)
    def _():
        copy = pltpu.make_async_copy(all_ref, f_ref.at[pl.ds(0, NP), :], sem.at[1])
        copy.start()
        copy.wait()

    @pl.when(~over)
    def _():
        for s in range(grid_rows):
            f_ref[pl.ds(s * cap_top, cap_top), :] = piece_refs[s][...]

    lower = mm(order_ref[...], moved_ref[...]).astype(jnp.bfloat16)
    update_rows(f_ref, lower, upper_ref, f_ref, lax.axis_index("col") < 2)

    def put(n, carry, base):
        t = owned_ref[n]
        slot = jnp.where(over, t, n + base)
        pltpu.make_async_copy(
            f_ref.at[pl.ds(slot, 1), :],
            out_ref.at[pl.ds(local_of(piv_ref[t], grid_rows), 1), :],
            sem.at[1],
        ).start()
        return carry

    for panel, low, high in ((0, jnp.int32(0), first), (1, first, total)):
        back = lax.rem(my_row - panel + grid_rows, grid_rows)
        lax.fori_loop(low, high, functools.partial(put, base=back * cap_top - low), 0)

    def wait(_, carry):
        pltpu.make_async_copy(
            f_ref.at[pl.ds(0, 1), :], out_ref.at[pl.ds(0, 1), :], sem.at[1]
        ).wait()
        return carry

    lax.fori_loop(0, total, wait, 0)

    @pl.when(my_row < 2)
    def _():
        pltpu.make_async_copy(top_ref, out_ref.at[pl.ds(0, NB), :], sem.at[0]).wait()


def place_moved(pieces, order, moved, upper, everything, top, result, pivots, owned, over):
    grid_rows = len(pieces)
    cols = result.shape[1]
    smem = pl.BlockSpec(memory_space=pltpu.SMEM)
    vmem = pl.BlockSpec(memory_space=pltpu.VMEM)
    anywhere = pl.BlockSpec(memory_space=pl.ANY)
    return pl.pallas_call(
        functools.partial(place_kernel, grid_rows),
        out_shape=jax.ShapeDtypeStruct(result.shape, result.dtype),
        in_specs=[smem] * 3 + [vmem] * (grid_rows + 3) + [anywhere] * 3,
        out_specs=anywhere,
        input_output_aliases={grid_rows + 8: 0},
        scratch_shapes=[
            pltpu.VMEM((order.shape[0], cols), jnp.float32),
            pltpu.SemaphoreType.DMA((2,)),
        ],
        compiler_params=pltpu.CompilerParams(vmem_limit_bytes=24 * MIB),
        name="place_moved",
    )(over, pivots, owned, *pieces, order, moved, upper, everything, top, result)


def merge_kernel(bits, arrived1, arrived2, held1, held2, _, out_ref):
    chip = lax.div(lax.axis_index("col"), 2)
    size = held1.shape[0]
    for k, (bit, arrived, held) in enumerate(zip(bits, (arrived1, arrived2), (held1, held2))):
        here = pl.ds(k * size, size)
        came = (chip & bit) != 0

        @pl.when(came)
        def _(arrived=arrived, here=here):
            out_ref[here, :] = arrived[...]

        @pl.when(~came)
        def _(held=held, here=here):
            out_ref[here, :] = held[...]


def merge(bits, arrived, held, after):
    size = held[0].shape[0]
    vmem = pl.BlockSpec(memory_space=pltpu.VMEM)
    return pl.pallas_call(
        functools.partial(merge_kernel, bits),
        out_shape=jax.ShapeDtypeStruct((2 * size, LANES), jnp.float32),
        in_specs=[vmem] * 4 + [pl.BlockSpec(memory_space=pl.ANY)],
        out_specs=vmem,
        compiler_params=pltpu.CompilerParams(vmem_limit_bytes=16 * MIB),
        name="merge",
    )(*arrived, *held, after)


def spread_round(value, bit, reached):
    pairs = [(2 * c + k, 2 * (c | bit) + k) for c in reached for k in range(2)]
    return lax.ppermute(value, "col", pairs)


def shards(matrix, pivots):
    grid_rows = lax.axis_size("row")
    grid_cols = lax.axis_size("col")
    chips = grid_cols // 2
    assert grid_rows > 1 and chips * 2 == grid_cols and not chips & (chips - 1)
    my_row = lax.axis_index("row")
    my_chip = lax.axis_index("col") // 2
    cap, cap_top = capacities(grid_rows)
    flat = pivots.reshape(-1)
    swap = [(c, c ^ 1) for c in range(grid_cols)]
    bits = [1 << b for b in range(chips.bit_length() - 1)]

    halves = pack_panel(matrix)
    rows, corner, owned, unwritten = gather_rows(matrix, flat, halves[0], cap, grid_rows)
    all_rows = lax.all_gather(rows, "row", tiled=True)

    shifts = [[(r, (r + s) % grid_rows) for r in range(grid_rows)] for s in range(1, grid_rows)]
    corner = corner + sum(lax.ppermute(corner, "row", shift) for shift in shifts)
    corner = jnp.where(my_chip == 0, corner, 0.0) + sum(
        lax.ppermute(corner, "col", [(0, 2 * chip), (1, 2 * chip + 1)]) for chip in range(1, chips)
    )
    corner_other = lax.ppermute(corner, "col", swap)

    owner = owner_of(flat, grid_rows)
    number = jnp.arange(NP, dtype=jnp.int32)
    panel = number // NB
    same = owner[:, None] == owner[None, :]
    alike = same & (panel[None, :] == panel[:, None])
    before = number[None, :] < number[:, None]
    rank = jnp.sum(same & before, axis=1, dtype=jnp.int32)
    panel_rank = jnp.sum(alike & before, axis=1, dtype=jnp.int32)
    over = jnp.max(jnp.maximum(rank - cap, panel_rank - cap_top)) >= 0
    position = jnp.where(over, number, owner * cap + rank)
    order = position[:, None] == jnp.arange(grid_rows * cap, dtype=jnp.int32)[None, :]
    order = order.astype(jnp.bfloat16)
    back = (my_row - panel + grid_rows) % grid_rows
    slot = jnp.where(over, number, back * cap_top + panel_rank)
    slots = jnp.arange(grid_rows * cap_top, dtype=jnp.int32)
    order_top = (slot[None, :] == slots[:, None]) & (owner == my_row)[None, :]
    order_top = order_top.astype(jnp.bfloat16)
    over = over.astype(jnp.int32)
    over_list = over.reshape(1)

    quarter = halves[0].shape[0]
    held = halves
    reached = ([0], [0])
    for step, both in enumerate(zip(bits, bits[::-1])):
        arrived = [spread_round(v, bit, r) for v, bit, r in zip(held, both, reached)]
        reached = [r + [c | bit for c in r] for bit, r in zip(both, reached)]
        if step + 1 == len(bits):
            lu, linv, weights, moved = factor_corner(corner, corner_other, order, held[0])
        own = merge(both, arrived, held, corner if step + 1 < len(bits) else lu)
        held = (own[:quarter], own[quarter:])
    other = lax.ppermute(own, "col", swap)

    tops = top_rows(matrix, flat, lu, cap_top, grid_rows)
    pieces = [tops[0]]
    for s in range(1, grid_rows):
        pairs = [(c, (c + s) % grid_rows) for c in range(2)]
        pieces.append(lax.ppermute(tops[s], "row", pairs))
    def sum_rows(state):
        mine = owner == my_row
        local = jnp.where(mine, local_of(flat, grid_rows), 0)
        picked = jnp.where(mine[:, None], matrix[local], 0.0)
        tops = jnp.where((panel == my_row)[:, None], matrix[number % NB], 0.0)
        picked, tops = lax.psum((picked, tops), "row")
        return jnp.int32(0), jnp.zeros_like(state[1]).at[:NP].set(picked), tops

    _, all_rows, summed_tops = lax.while_loop(
        lambda state: state[0] > 0, sum_rows, (over, all_rows, unwritten)
    )

    upper, top = upper_rows_of(all_rows, linv, lu)
    lower = lower_rows(own, other, weights)
    result = trailing(matrix, lower, upper)
    return place_moved(
        pieces, order_top, moved, upper, summed_tops, top, result, flat, owned, over_list
    )


def solution(mesh):
    placed = (P("row", "col"), P())
    return jax.shard_map(
        shards, mesh=mesh, in_specs=placed, out_specs=P("row", "col"), check_vma=False
    )
```
